256 devices in a mesh: dom: 128 (over x, y_hi, z, core), feat: 2 (over y_lo).
Axes of the slice: x: 4, y: 4 (y_hi: 2, y_lo: 2; y = y_hi * 2 + y_lo), z: 8, core: 2. Of those that a mesh axis runs over, the one named last changes fastest.
Arguments:
- features: float32 [131072, 512], P('dom', 'feat'), may hold values from -6 to 6
- weight: float32 [512, 512], P(None, 'feat'), may hold values from -0.25 to 0.25
- cotangent: float32 [131072, 512], P('dom', 'feat'), may hold values from -6 to 6
- block_rows: int32 [128, 4, 24], P('dom'), may hold values from 0 to 7, as said below
- block_cols: int32 [128, 4, 24], P('dom'), may hold values from 0 to 7, as said below
- block_counts: int32 [128, 4], P('dom'), may hold values from 1 to 24, as said below
- block_values: float32 [128, 4, 24, 128, 128], P('dom'), may hold values from -0.25 to 0.25
Outputs:
- activated: float32 [131072, 512], P('dom', 'feat')
- feature_grad: float32 [131072, 512], P('dom', 'feat')
- weight_grad: float32 [512, 512], P(None, 'feat')
The draws below stay inside these ranges and needn't reach their ends.
Inputs may be any that keep to these rules, and one draw needn't show every extreme that they name: `block_rows`: every entry is below 8; within one partition and slot the pairs (block_rows, block_cols) are all different. `block_cols`: every entry is below 8. `block_counts`: some partition has 24 blocks in every slot.
All inputs are finite; a program needn't handle non-finite values.
Results may differ from the reference program's by a relative error of at most 0.0003.
Values sent between devices are 32-bit elements; how exact they have to be, the bound alone decides.
A program may use at most 128 MiB of HBM per device.

```python
import math
import jax
import jax.numpy as jnp
from jax import lax

HID = 512
BLOCK = 128
WIN = 4
BLOCK_ROWS = 8
CAP = 24
PARTS_SIZE = 128
NODES = 131072


def block_pairs(key):
    subkeys = jax.random.split(key, PARTS_SIZE * WIN)

    def single_order(subkey):
        return jax.random.permutation(subkey, BLOCK_ROWS * BLOCK_ROWS)
    orders = jax.vmap(single_order)(subkeys)
    return orders[:, :CAP].reshape(PARTS_SIZE, WIN, CAP).astype(jnp.int32)


def draw_block_rows(key, part):
    pairs = block_pairs(key)
    return (pairs // BLOCK_ROWS).astype(jnp.int32)


def draw_block_cols(key, part):
    pairs = block_pairs(key)
    return (pairs % BLOCK_ROWS).astype(jnp.int32)


def draw_block_counts(key, part):
    key = jax.random.fold_in(key, 7)
    first_key, second_key, third_key = jax.random.split(key, 3)
    first = jax.random.randint(first_key, (PARTS_SIZE, WIN), 0, CAP)
    second = jax.random.randint(second_key, (PARTS_SIZE, WIN), 0, CAP + 1)
    counts = 1 + first * second // CAP
    busiest = jax.random.randint(third_key, (), 0, PARTS_SIZE)
    positions = jnp.arange(PARTS_SIZE, dtype=jnp.int32)[:, None]
    counts = jnp.where(positions == busiest, CAP, counts)
    return counts.astype(jnp.int32)


def levels(stream_key, dims, pieces, least, high):
    level = 1.0
    for axis_at, shards_of in pieces:
        draws = jax.random.uniform(jax.random.fold_in(jax.random.fold_in(stream_key, 6), axis_at), (shards_of,), jnp.float32, least / len(pieces), high / len(pieces))
        level = level * jnp.repeat(jnp.exp(draws), dims[axis_at] // shards_of).reshape((-1,) + (1,) * (len(dims) - 1 - axis_at))
    return level


def normal_values(own_key, extent, scale, reach, pieces=(), kind=jnp.bfloat16):
    loudness = levels(own_key, extent, pieces, -0.22, 0.18) if pieces else 1.0
    drawn = jax.random.normal(own_key, extent, jnp.float32) * scale * loudness
    return jnp.minimum(jnp.maximum(drawn, -reach), reach).astype(kind)


def setup_inputs(seed: int = 0) -> dict:
    splits = jax.random.split(jax.random.key(seed), 8)
    return {
        "features": normal_values(splits[0], (NODES, HID), 1.0, 6.0, ((0, 128), (1, 2)), jnp.float32),
        "weight": normal_values(splits[1], (HID, HID), HID ** -0.5, 0.25, ((1, 2),), jnp.float32),
        "cotangent": normal_values(splits[2], (NODES, HID), 1.0, 6.0, ((0, 128), (1, 2)), jnp.float32),
        "block_rows": draw_block_rows(jax.random.fold_in(splits[7], 71), 0),
        "block_cols": draw_block_cols(jax.random.fold_in(splits[7], 71), 0),
        "block_counts": draw_block_counts(jax.random.fold_in(splits[7], 71), 0),
        "block_values": normal_values(splits[6], (PARTS_SIZE, WIN, CAP, BLOCK, BLOCK), (4 * BLOCK) ** -0.5, 0.25, ((0, 128),), jnp.float32),
    }


def aggregate(dense, block_rows, block_cols, block_counts, block_values):
    width = dense.shape[1]
    grouped = dense.reshape(PARTS_SIZE, BLOCK_ROWS, BLOCK, width)
    live = (jnp.arange(CAP, dtype=jnp.int32)[None, None, :] < block_counts[:, :, None]).astype(jnp.float32)

    def one_part(part_index):
        total = jnp.zeros((BLOCK_ROWS, BLOCK, width), jnp.float32)
        for slot_index in range(WIN):
            source_index = ((part_index - slot_index) % PARTS_SIZE).astype(jnp.int32)
            source = lax.dynamic_index_in_dim(grouped, source_index, 0, keepdims=False)
            picked = source[block_cols[part_index, slot_index]]
            blocks = block_values[part_index, slot_index] * live[part_index, slot_index][:, None, None]
            product = jnp.einsum('cij,cjh->cih', blocks, picked, precision=lax.Precision.HIGHEST)
            total = total.at[block_rows[part_index, slot_index]].add(product)
        return total
    return lax.map(one_part, jnp.arange(PARTS_SIZE, dtype=jnp.int32)).reshape(NODES, width)

def reference(features, weight, cotangent, block_rows, block_cols, block_counts, block_values):

    def forward(inputs, matrix):
        hidden = jnp.dot(inputs, matrix, precision=lax.Precision.HIGHEST, preferred_element_type=jnp.float32)
        pre = aggregate(hidden, block_rows, block_cols, block_counts, block_values)
        return jax.nn.silu(pre)
    activated, pullback = jax.vjp(forward, features, weight)
    feature_grad, weight_grad = pullback(cotangent)
    weight_grad = weight_grad * jnp.float32(1.0 / math.sqrt(NODES))
    return (activated, feature_grad, weight_grad)
```

```python
import math

import jax
import jax.numpy as jnp
from jax import lax
from jax.experimental import pallas as pl
from jax.experimental.pallas import tpu as pltpu
from jax.sharding import PartitionSpec as P

MESH = pl.DeviceIdType.MESH
F32 = jnp.float32
BF16 = jnp.bfloat16
X, Y, Z, CORES = 4, 2, 8, 2
PARTS = X * Y * Z * CORES
SLOTS, CAP, GRID = 4, 24, 8
ROWS, HALF, LANES = 1024, 256, 128


def split(value):
    high = value.astype(BF16)
    return high, (value - high.astype(F32)).astype(BF16)


def dot(a, b):
    return jnp.dot(a, b, preferred_element_type=F32)


def dot3(a, b):
    return dot(a[0], b[0]) + dot(a[1], b[0]) + dot(a[0], b[1])


def remote(src, dst, send, recv, device):
    return pltpu.make_async_remote_copy(
        src_ref=src, dst_ref=dst, send_sem=send, recv_sem=recv,
        device_id=device, device_id_type=MESH,
    )


def kernel(
    table, features, weight, cotangent, blocks_in,
    act_out, grad_out, wgrad_out,
    blocks, adj_hi, adj_lo, own, w_raw, w_hi, w_lo, wt_hi, wt_lo, cot,
    fwd, agg, agg_far, pre, act, pgt_hi, pgt_lo,
    z_send, z_recv, f_send, f_recv, f_own,
    ar, ar_core, s1, ar_x, s2, ar_y, s3, ar_z, ag, wg,
    local_sem, fwd_ss, fwd_rs, y_ss, y_rs, z_ss, z_rs, f_ss, f_rs,
    ar_ss, ar_rs, ag_ss, ag_rs,
):
    me = lax.axis_index("dom")
    feat = lax.axis_index("feat")
    other = 1 - feat
    core = lax.rem(me, 2)
    z = lax.rem(me // 2, Z)
    y = lax.rem(me // (2 * Z), Y)
    x = me // (2 * Z * Y)
    up = (lax.rem(me + 1, PARTS), feat)
    down = (lax.rem(me + PARTS - 1, PARTS), feat)
    mate = (me, other)

    def at(x_, y_, z_, core_):
        return (((x_ * Y + y_) * Z + z_) * 2 + core_, feat)

    core_peer = at(x, y, z, 1 - core)
    y_peer = at(x, 1 - y, z, core)

    def x_peer(d):
        return lax.rem(x + d, X)

    def z_peer(d):
        return lax.rem(z + d, Z)

    loads = [
        pltpu.make_async_copy(blocks_in, blocks, local_sem.at[0]),
        pltpu.make_async_copy(features, own, local_sem.at[1]),
        pltpu.make_async_copy(weight, w_raw, local_sem.at[2]),
        pltpu.make_async_copy(cotangent, cot, local_sem.at[3]),
    ]
    for load in loads:
        load.start()

    barrier = pltpu.get_barrier_semaphore()
    partners = [up, down, mate, y_peer]
    partners += [at(x_peer(d), y, z, core) for d in range(1, X)]
    partners += [at(x, y, z_peer(d), core) for d in range(1, Z)]
    for partner in partners:
        pl.semaphore_signal(barrier, inc=1, device_id=partner, device_id_type=MESH)
    pl.semaphore_wait(barrier, len(partners))

    def fwd_at(w, c, j):
        return ((w - 1) * 2 + c) * 4 + j

    def fwd_copy(w, c, j):
        i = fwd_at(w, c, j)
        if w == 1:
            src = features.at[pl.ds(j * 256, 256), pl.ds(c * LANES, LANES)]
        else:
            src = fwd.at[fwd_at(w - 1, c, j)]
        return remote(src, fwd.at[i], fwd_ss.at[i], fwd_rs.at[i], up)

    def each(n, body, start=0):
        def step(j, carry):
            body(j)
            return carry

        lax.fori_loop(start, start + n, step, 0)

    def send_own(c):
        for j in range(4):
            fwd_copy(1, c, j).start()

    def pass_on(w, c):
        def body(j):
            fwd_copy(w, c, j).wait_recv()
            fwd_copy(w + 1, c, j).start()

        each(4, body)

    def densify(w):
        def body(r):
            rows = pl.ds(pl.multiple_of(r * LANES, LANES), LANES)
            for c in range(GRID):
                found = table[(w * GRID + r) * GRID + c]
                live = jnp.where(found >= 0, 1.0, 0.0).astype(F32)
                high, low = split(blocks[w * CAP + jnp.maximum(found, 0)] * live)
                adj_hi[w * GRID + c, rows, :] = high
                adj_lo[w * GRID + c, rows, :] = low

        each(GRID, body)

    def gather_in(w, c, j, piece, first=False, last=None):
        high, low = split(piece)
        both = jnp.concatenate([high, low], axis=1)

        def body(i):
            rows = pl.ds(pl.multiple_of(i * 512, 512), 512)
            a_hi = jnp.concatenate(
                [adj_hi[w * GRID + 2 * j, rows, :], adj_hi[w * GRID + 2 * j + 1, rows, :]], axis=1
            )
            a_lo = jnp.concatenate(
                [adj_lo[w * GRID + 2 * j, rows, :], adj_lo[w * GRID + 2 * j + 1, rows, :]], axis=1
            )
            wide = dot(a_hi, both)
            total = wide[:, :LANES] + wide[:, LANES:] + dot(a_lo, high)
            if first:
                agg[c, rows, :] = total
            else:
                agg[c, rows, :] += total
            if last is not None:
                last(i)

        each(2, body)

    def gather_own(c):
        def piece(j):
            rows = pl.ds(pl.multiple_of(j * 256, 256), 256)
            return own[rows, pl.ds(c * LANES, LANES)]

        gather_in(0, c, 0, piece(0), first=True)
        each(3, lambda j: gather_in(0, c, j, piece(j)), 1)

    def gather_slot(w, c, wait, n=4):
        def body(j):
            if wait:
                fwd_copy(w, c, j).wait_recv()
            gather_in(w, c, j, fwd[fwd_at(w, c, j)])

        each(n, body)

    def y_copy(c, i):
        rows = pl.ds(pl.multiple_of(i * 512, 512), 512)
        n = c * 2 + i
        return remote(agg.at[c, rows], agg_far.at[c, rows], y_ss.at[n], y_rs.at[n], mate)

    def gather_last(c):
        gather_slot(3, c, True, 3)
        fwd_copy(3, c, 3).wait_recv()
        gather_in(3, c, 3, fwd[fwd_at(3, c, 3)], last=lambda i: y_copy(c, i).start())

    send_own(0)
    loads[0].wait()
    densify(0)
    densify(1)
    pass_on(1, 0)
    densify(2)
    pass_on(2, 0)
    send_own(1)
    densify(3)
    loads[1].wait()
    gather_own(0)
    gather_slot(1, 0, False)
    gather_slot(2, 0, False)
    pass_on(1, 1)
    gather_last(0)
    pass_on(2, 1)
    gather_own(1)
    gather_slot(1, 1, False)
    gather_slot(2, 1, False)

    loads[2].wait()
    for k in range(2):
        value = w_raw[pl.ds(k * HALF, HALF), :]
        w_hi[k], w_lo[k] = split(value)
        wt_hi[k], wt_lo[k] = split(value.T)
    loads[3].wait()
    gather_last(1)

    def near_part(i):
        rows = pl.ds(pl.multiple_of(i * 256, 256), 256)
        value = jnp.concatenate([agg[0, rows, :], agg[1, rows, :]], axis=1)
        pre[rows, :] = dot3(split(value), (w_hi[feat], w_lo[feat]))

    each(4, near_part)
    for i in range(2):
        y_copy(0, i).wait_recv()

    def far_part(c, i):
        rows = pl.ds(pl.multiple_of(i * 256, 256), 256)
        ks = pl.ds(c * LANES, LANES)
        return dot3(split(agg_far[c, rows, :]), (w_hi[other, ks, :], w_lo[other, ks, :]))

    def far_first(i):
        rows = pl.ds(pl.multiple_of(i * 256, 256), 256)
        pre[rows, :] += far_part(0, i)

    each(4, far_first)

    def activate(i):
        rows = pl.ds(pl.multiple_of(i * 256, 256), 256)
        value = pre[rows, :] + far_part(1, i)
        s = jax.nn.sigmoid(value)
        act[rows, :] = value * s
        grad = cot[rows, :] * (s + value * s * (1.0 - s))
        pgt_hi[:, rows], pgt_lo[:, rows] = split(grad.T)

    for i in range(2):
        y_copy(1, i).wait_recv()
        each(2, activate, 2 * i)
    act_copy = pltpu.make_async_copy(act, act_out, local_sem.at[4])
    act_copy.start()

    def term(w, j):
        n = w * GRID + j
        high, low = pgt_hi[...], pgt_lo[...]
        return dot(high, adj_hi[n]) + dot(low, adj_hi[n]) + dot(high, adj_lo[n])

    def z_copy(s, j):
        n = s * GRID + j
        return remote(z_send.at[n], z_recv.at[n], z_ss.at[n], z_rs.at[n], down)

    def z_step(s, j):
        value = term(3 - s, j)
        if s > 0:
            z_copy(s - 1, j).wait_recv()
            value = value + z_recv[(s - 1) * GRID + j]
        z_send[s * GRID + j] = value
        z_copy(s, j).start()

    def f_copy(j):
        return remote(f_send.at[j], f_recv.at[j], f_ss.at[j], f_rs.at[j], mate)

    def last_step(j):
        value = term(0, j)
        z_copy(2, j).wait_recv()
        value = value + z_recv[2 * GRID + j]
        parts = split(value.T)
        f_send[j] = dot3(parts, (wt_hi[other], wt_lo[other]))
        f_copy(j).start()
        f_own[j] = dot3(parts, (wt_hi[feat], wt_lo[feat]))

    scale = F32(1.0 / math.sqrt(ROWS * PARTS))

    def weight_part(source, half, c):
        grad = dot3((pgt_hi[...], pgt_lo[...]), split(source[c])).T * scale
        for h in range(2):
            start = pl.multiple_of(h * 512 + half * HALF + c * LANES, LANES)
            ar[pl.ds(start, LANES), :] = grad[:, h * LANES:(h + 1) * LANES]

    def rows_at(start, size, ref):
        return ref.at[pl.ds(pl.multiple_of(start, 8), size)]

    def read_at(start, size, ref):
        return ref[pl.ds(pl.multiple_of(start, 8), size), :]

    def sum_core():
        return remote(rows_at((1 - core) * 512, 512, ar), ar_core, ar_ss.at[0], ar_rs.at[0], core_peer)

    def sum_x(d):
        return remote(
            rows_at(x_peer(d) * 128, 128, s1), ar_x.at[d - 1], ar_ss.at[d], ar_rs.at[d],
            at(x_peer(d), y, z, core),
        )

    def sum_y():
        return remote(rows_at((1 - y) * 64, 64, s2), ar_y, ar_ss.at[4], ar_rs.at[4], y_peer)

    def sum_z(d):
        return remote(
            rows_at(z_peer(d) * 8, 8, s3), ar_z.at[d - 1], ar_ss.at[4 + d], ar_rs.at[4 + d],
            at(x, y, z_peer(d), core),
        )

    base_core = core * 512
    base_x = base_core + x * 128
    base_y = base_x + y * 64
    base_z = base_y + z * 8

    def share(base, size, n, device):
        return remote(rows_at(base, size, ag), rows_at(base, size, ag), ag_ss.at[n], ag_rs.at[n], device)

    def share_z(d):
        return share(base_z, 8, d - 1, at(x, y, z_peer(d), core))

    def share_y():
        return share(base_y, 64, 7, y_peer)

    def share_x(d):
        return share(base_x, 128, 7 + d, at(x_peer(d), y, z, core))

    def share_core():
        return share(base_core, 512, 11, core_peer)

    def landed_z(d):
        peer = lax.rem(z + Z - d, Z)
        return share(base_y + peer * 8, 8, d - 1, mate)

    def landed_y():
        return share(base_x + (1 - y) * 64, 64, 7, mate)

    def landed_x(d):
        peer = lax.rem(x + X - d, X)
        return share(base_core + peer * 128, 128, 7 + d, mate)

    def landed_core():
        return share((1 - core) * 512, 512, 11, mate)

    def point0():
        sum_core().start()

    def point1():
        sum_core().wait_recv()
        s1[...] = read_at(base_core, 512, ar) + ar_core[...]
        for d in range(1, X):
            sum_x(d).start()

    def point2():
        total = read_at(x * 128, 128, s1)
        for d in range(1, X):
            sum_x(d).wait_recv()
            total = total + ar_x[d - 1]
        s2[...] = total
        sum_y().start()

    def point3():
        sum_y().wait_recv()
        s3[...] = read_at(y * 64, 64, s2) + ar_y[...]
        for d in range(1, Z):
            sum_z(d).start()

    def point4():
        total = read_at(z * 8, 8, s3)
        for d in range(1, Z):
            sum_z(d).wait_recv()
            total = total + ar_z[d - 1]
        ag[pl.ds(pl.multiple_of(base_z, 8), 8), :] = total
        for d in range(1, Z):
            share_z(d).start()

    def point5():
        for d in range(1, Z):
            landed_z(d).wait_recv()
        share_y().start()

    def point6():
        landed_y().wait_recv()
        for d in range(1, X):
            share_x(d).start()

    def point7():
        for d in range(1, X):
            landed_x(d).wait_recv()
        share_core().start()

    wgrad_copy = pltpu.make_async_copy(wg, wgrad_out, local_sem.at[5])

    def point8():
        landed_core().wait_recv()
        for h in range(2):
            wg[:, h * LANES:(h + 1) * LANES] = ag[pl.ds(h * 512, 512), :]
        wgrad_copy.start()

    each(GRID, lambda j: z_step(0, j))
    for c in range(2):
        weight_part(agg, feat, c)
        weight_part(agg_far, other, c)
    point0()
    each(4, lambda j: z_step(1, j))
    point1()
    each(4, lambda j: z_step(1, j), 4)
    point2()
    each(4, lambda j: z_step(2, j))
    point3()
    each(4, lambda j: z_step(2, j), 4)
    point4()
    each(2, last_step)
    point5()
    each(2, last_step, 2)
    point6()
    each(2, last_step, 4)
    point7()
    each(2, last_step, 6)
    point8()

    def finish(j):
        f_copy(j).wait_recv()
        f_own[j] += f_recv[j]
        rows = pl.ds(pl.multiple_of(j * LANES, LANES), LANES)
        pltpu.make_async_copy(f_own.at[j], grad_out.at[rows], local_sem.at[6 + j]).start()

    each(GRID, finish)

    for c in range(2):
        for w in range(1, SLOTS):
            for j in range(4):
                fwd_copy(w, c, j).wait_send()
        for i in range(2):
            y_copy(c, i).wait_send()

    def sent(j):
        for s in range(3):
            z_copy(s, j).wait_send()
        f_copy(j).wait_send()

    each(GRID, sent)
    sum_core().wait_send()
    sum_y().wait_send()
    share_core().wait_send()
    share_y().wait_send()
    for d in range(1, X):
        sum_x(d).wait_send()
        share_x(d).wait_send()
    for d in range(1, Z):
        sum_z(d).wait_send()
        share_z(d).wait_send()
    act_copy.wait()
    wgrad_copy.wait()

    def written(j):
        rows = pl.ds(pl.multiple_of(j * LANES, LANES), LANES)
        pltpu.make_async_copy(f_own.at[j], grad_out.at[rows], local_sem.at[6 + j]).wait()

    each(GRID, written)


def body(features, weight, cotangent, block_rows, block_cols, block_counts, block_values):
    order = jnp.arange(CAP, dtype=jnp.int32)
    live = order[None, :] < block_counts[0][:, None]
    place = jnp.where(live, block_rows[0] * GRID + block_cols[0], -1)
    hit = place[:, None, :] == jnp.arange(GRID * GRID, dtype=jnp.int32)[None, :, None]
    table = jnp.max(jnp.where(hit, order[None, None, :], -1), axis=2).reshape(-1)
    vmem = pltpu.VMEM
    dma = pltpu.SemaphoreType.DMA
    anywhere = pl.BlockSpec(memory_space=pl.ANY)
    return pl.pallas_call(
        kernel,
        out_shape=(
            jax.ShapeDtypeStruct((ROWS, HALF), F32),
            jax.ShapeDtypeStruct((ROWS, HALF), F32),
            jax.ShapeDtypeStruct((2 * HALF, HALF), F32),
        ),
        in_specs=[pl.BlockSpec(memory_space=pltpu.SMEM)] + [anywhere] * 4,
        out_specs=(anywhere,) * 3,
        scratch_shapes=[
            vmem((SLOTS * CAP, LANES, LANES), F32),
            vmem((SLOTS * GRID, ROWS, LANES), BF16),
            vmem((SLOTS * GRID, ROWS, LANES), BF16),
            vmem((ROWS, HALF), F32),
            vmem((2 * HALF, HALF), F32),
            vmem((2, HALF, HALF), BF16),
            vmem((2, HALF, HALF), BF16),
            vmem((2, HALF, HALF), BF16),
            vmem((2, HALF, HALF), BF16),
            vmem((ROWS, HALF), F32),
            vmem((24, 256, LANES), F32),
            vmem((2, ROWS, LANES), F32),
            vmem((2, ROWS, LANES), F32),
            vmem((ROWS, HALF), F32),
            vmem((ROWS, HALF), F32),
            vmem((HALF, ROWS), BF16),
            vmem((HALF, ROWS), BF16),
            vmem((3 * GRID, HALF, LANES), F32),
            vmem((3 * GRID, HALF, LANES), F32),
            vmem((GRID, LANES, HALF), F32),
            vmem((GRID, LANES, HALF), F32),
            vmem((GRID, LANES, HALF), F32),
            vmem((1024, LANES), F32),
            vmem((512, LANES), F32),
            vmem((512, LANES), F32),
            vmem((3, 128, LANES), F32),
            vmem((128, LANES), F32),
            vmem((64, LANES), F32),
            vmem((64, LANES), F32),
            vmem((7, 8, LANES), F32),
            vmem((1024, LANES), F32),
            vmem((2 * HALF, HALF), F32),
            dma((14,)),
            dma((24,)), dma((24,)),
            dma((4,)), dma((4,)),
            dma((24,)), dma((24,)),
            dma((8,)), dma((8,)),
            dma((12,)), dma((12,)),
            dma((12,)), dma((12,)),
        ],
        compiler_params=pltpu.CompilerParams(
            collective_id=0, has_side_effects=True, vmem_limit_bytes=56 * 2**20
        ),
        cost_estimate=pl.CostEstimate(flops=16 * 10**9, bytes_accessed=12 * 2**20, transcendentals=ROWS * HALF),
        name="layer",
    )(table, features, weight, cotangent, block_values.reshape(SLOTS * CAP, LANES, LANES))


def solution(mesh):
    in_specs = (
        P("dom", "feat"),
        P(None, "feat"),
        P("dom", "feat"),
        P("dom", None, None),
        P("dom", None, None),
        P("dom", None),
        P("dom", None, None, None, None),
    )
    out_specs = (P("dom", "feat"), P("dom", "feat"), P(None, "feat"))
    return jax.shard_map(body, mesh=mesh, in_specs=in_specs, out_specs=out_specs, check_vma=False)
```

```python
import math

import jax
import jax.numpy as jnp
from jax import lax
from jax.experimental import pallas as pl
from jax.experimental.pallas import tpu as pltpu
from jax.sharding import PartitionSpec as P

MESH = pl.DeviceIdType.MESH
F32 = jnp.float32
BF16 = jnp.bfloat16
X, Y, Z, CORES = 4, 2, 8, 2
PARTS = X * Y * Z * CORES
SLOTS, CAP, GRID = 4, 24, 8
ROWS, HALF, LANES = 1024, 256, 128


def split(value):
    high = value.astype(BF16)
    return high, (value - high.astype(F32)).astype(BF16)


def dot(a, b):
    return jnp.dot(a, b, preferred_element_type=F32)


def dot3(a, b):
    return dot(a[0], b[0]) + dot(a[1], b[0]) + dot(a[0], b[1])


def remote(src, dst, send, recv, device):
    return pltpu.make_async_remote_copy(
        src_ref=src, dst_ref=dst, send_sem=send, recv_sem=recv,
        device_id=device, device_id_type=MESH,
    )


def kernel(
    table, features, weight, cotangent, blocks_in,
    act_out, grad_out, wgrad_out,
    blocks, adj_hi, adj_lo, own, w_raw, w_hi, w_lo, wt_hi, wt_lo, cot,
    fwd, agg, agg_far, pre, act, pgt_hi, pgt_lo,
    z_send, z_recv, f_send, f_recv, f_own,
    ar, ar_core, s1, ar_x, s2, ar_y, s3, ar_z, ag, wg,
    fwd_relay, z_relay,
    local_sem, fwd_ss, fwd_rs, y_ss, y_rs, z_ss, z_rs, f_ss, f_rs,
    fwd_in, fwd_on, z_in, z_on,
    ar_ss, ar_rs, ag_ss, ag_rs,
):
    me = lax.axis_index("dom")
    feat = lax.axis_index("feat")
    other = 1 - feat
    core = lax.rem(me, 2)
    z = lax.rem(me // 2, Z)
    y = lax.rem(me // (2 * Z), Y)
    x = me // (2 * Z * Y)
    up = (lax.rem(me + 1, PARTS), feat)
    down = (lax.rem(me + PARTS - 1, PARTS), feat)
    mate = (me, other)

    def at(x_, y_, z_, core_):
        return (((x_ * Y + y_) * Z + z_) * 2 + core_, feat)

    core_peer = at(x, y, z, 1 - core)
    x_next, x_before = lax.rem(x + y, X), lax.rem(x + y + X - 1, X)
    first_z, last_z = z == 0, z == Z - 1
    is_odd, is_even = core == 1, core == 0
    wraps_up, wraps_down = is_odd & last_z, is_even & first_z
    relays_up, relays_down = is_even & last_z, is_odd & first_z
    up_relay = at(x_next, 1 - y, Z - 1, 0)
    up_relay_on = at(x, y, 0, 0)
    down_relay = at(x_before, 1 - y, 0, 1)
    down_relay_on = at(x, y, Z - 1, 1)
    y_peer = at(x, 1 - y, z, core)

    def x_peer(d):
        return lax.rem(x + d, X)

    def z_peer(d):
        return lax.rem(z + d, Z)

    loads = [
        pltpu.make_async_copy(blocks_in, blocks, local_sem.at[0]),
        pltpu.make_async_copy(features, own, local_sem.at[1]),
        pltpu.make_async_copy(weight, w_raw, local_sem.at[2]),
        pltpu.make_async_copy(cotangent, cot, local_sem.at[3]),
    ]
    for load in loads:
        load.start()

    barrier = pltpu.get_barrier_semaphore()
    partners = [up, down, mate, y_peer]
    partners += [at(x_peer(d), y, z, core) for d in range(1, X)]
    partners += [at(x, y, z_peer(d), core) for d in range(1, Z)]
    partners += [at(x_next, 1 - y, z, 1 - core), at(x_before, 1 - y, z, 1 - core)]
    for partner in partners:
        pl.semaphore_signal(barrier, inc=1, device_id=partner, device_id_type=MESH)
    pl.semaphore_wait(barrier, len(partners))

    def fwd_at(w, c, j):
        return ((w - 1) * 2 + c) * 4 + j

    def fwd_copy(w, c, j):
        i = fwd_at(w, c, j)
        if w == 1:
            src = features.at[pl.ds(j * 256, 256), pl.ds(c * LANES, LANES)]
        else:
            src = fwd.at[fwd_at(w - 1, c, j)]
        return remote(src, fwd.at[i], fwd_ss.at[i], fwd_rs.at[i], up)

    def fwd_detour(w, c, j):
        i = fwd_at(w, c, j)
        if w == 1:
            src = features.at[pl.ds(j * 256, 256), pl.ds(c * LANES, LANES)]
        else:
            src = fwd.at[fwd_at(w - 1, c, j)]
        n = fwd_at(w, c, 0) // 2 + j // 2
        return remote(src, fwd_relay.at[n], fwd_ss.at[i], fwd_in.at[n], up_relay)

    def fwd_resend(w, c, j):
        i = fwd_at(w, c, j)
        n = fwd_at(w, c, 0) // 2 + j // 2
        return remote(fwd_relay.at[n], fwd.at[i], fwd_on.at[n], fwd_rs.at[i], up_relay_on)

    def fwd_start(w, c, j):
        if j % 2 == 0:
            fwd_copy(w, c, j).start()
        else:
            pl.when(wraps_up)(lambda: fwd_detour(w, c, j).start())
            pl.when(jnp.logical_not(wraps_up))(lambda: fwd_copy(w, c, j).start())

    def relay_up(w, c):
        def run():
            for j in (1, 3):
                fwd_detour(w, c, j).wait_recv()
                fwd_resend(w, c, j).start()

        pl.when(relays_up)(run)

    def each(n, body, start=0):
        def step(j, carry):
            body(j)
            return carry

        lax.fori_loop(start, start + n, step, 0)

    def send_own(c):
        for j in range(4):
            fwd_start(1, c, j)

    def pass_on(w, c):
        for j in range(4):
            fwd_copy(w, c, j).wait_recv()
            fwd_start(w + 1, c, j)

    def densify(w):
        def body(r):
            rows = pl.ds(pl.multiple_of(r * LANES, LANES), LANES)
            for c in range(GRID):
                found = table[(w * GRID + r) * GRID + c]
                live = jnp.where(found >= 0, 1.0, 0.0).astype(F32)
                high, low = split(blocks[w * CAP + jnp.maximum(found, 0)] * live)
                adj_hi[w * GRID + c, rows, :] = high
                adj_lo[w * GRID + c, rows, :] = low

        each(GRID, body)

    def gather_in(w, c, j, piece, first=False, last=None):
        high, low = split(piece)
        both = jnp.concatenate([high, low], axis=1)

        def body(i):
            rows = pl.ds(pl.multiple_of(i * 512, 512), 512)
            a_hi = jnp.concatenate(
                [adj_hi[w * GRID + 2 * j, rows, :], adj_hi[w * GRID + 2 * j + 1, rows, :]], axis=1
            )
            a_lo = jnp.concatenate(
                [adj_lo[w * GRID + 2 * j, rows, :], adj_lo[w * GRID + 2 * j + 1, rows, :]], axis=1
            )
            wide = dot(a_hi, both)
            total = wide[:, :LANES] + wide[:, LANES:] + dot(a_lo, high)
            if first:
                agg[c, rows, :] = total
            else:
                agg[c, rows, :] += total
            if last is not None:
                last(i)

        each(2, body)

    def gather_own(c):
        def piece(j):
            rows = pl.ds(pl.multiple_of(j * 256, 256), 256)
            return own[rows, pl.ds(c * LANES, LANES)]

        gather_in(0, c, 0, piece(0), first=True)
        each(3, lambda j: gather_in(0, c, j, piece(j)), 1)

    def gather_slot(w, c, wait, n=4):
        def body(j):
            if wait:
                fwd_copy(w, c, j).wait_recv()
            gather_in(w, c, j, fwd[fwd_at(w, c, j)])

        each(n, body)

    def y_copy(c, i):
        rows = pl.ds(pl.multiple_of(i * 512, 512), 512)
        n = c * 2 + i
        return remote(agg.at[c, rows], agg_far.at[c, rows], y_ss.at[n], y_rs.at[n], mate)

    def gather_last(c):
        gather_slot(3, c, True, 3)
        fwd_copy(3, c, 3).wait_recv()
        gather_in(3, c, 3, fwd[fwd_at(3, c, 3)], last=lambda i: y_copy(c, i).start())

    send_own(0)
    loads[0].wait()
    densify(0)
    densify(1)
    relay_up(1, 0)
    pass_on(1, 0)
    densify(2)
    densify(3)
    relay_up(2, 0)
    pass_on(2, 0)
    send_own(1)
    relay_up(3, 0)
    loads[1].wait()
    gather_own(0)
    gather_slot(1, 0, False)
    relay_up(1, 1)
    gather_slot(2, 0, False)
    gather_last(0)
    relay_up(2, 1)
    pass_on(1, 1)
    gather_own(1)
    relay_up(3, 1)
    pass_on(2, 1)
    gather_slot(1, 1, False)
    gather_slot(2, 1, False)

    loads[2].wait()
    for k in range(2):
        value = w_raw[pl.ds(k * HALF, HALF), :]
        w_hi[k], w_lo[k] = split(value)
        wt_hi[k], wt_lo[k] = split(value.T)
    loads[3].wait()
    gather_last(1)

    def near_part(i):
        rows = pl.ds(pl.multiple_of(i * 256, 256), 256)
        value = jnp.concatenate([agg[0, rows, :], agg[1, rows, :]], axis=1)
        pre[rows, :] = dot3(split(value), (w_hi[feat], w_lo[feat]))

    each(4, near_part)
    for i in range(2):
        y_copy(0, i).wait_recv()

    def far_part(c, i):
        rows = pl.ds(pl.multiple_of(i * 256, 256), 256)
        ks = pl.ds(c * LANES, LANES)
        return dot3(split(agg_far[c, rows, :]), (w_hi[other, ks, :], w_lo[other, ks, :]))

    def far_first(i):
        rows = pl.ds(pl.multiple_of(i * 256, 256), 256)
        pre[rows, :] += far_part(0, i)

    each(4, far_first)

    def activate(i):
        rows = pl.ds(pl.multiple_of(i * 256, 256), 256)
        value = pre[rows, :] + far_part(1, i)
        s = jax.nn.sigmoid(value)
        act[rows, :] = value * s
        grad = cot[rows, :] * (s + value * s * (1.0 - s))
        pgt_hi[:, rows], pgt_lo[:, rows] = split(grad.T)

    for i in range(2):
        y_copy(1, i).wait_recv()
        each(2, activate, 2 * i)
    act_copy = pltpu.make_async_copy(act, act_out, local_sem.at[4])
    act_copy.start()

    def term(w, j):
        n = w * GRID + j
        high, low = pgt_hi[...], pgt_lo[...]
        return dot(high, adj_hi[n]) + dot(low, adj_hi[n]) + dot(high, adj_lo[n])

    def z_copy(s, j):
        n = s * GRID + j
        return remote(z_send.at[n], z_recv.at[n], z_ss.at[n], z_rs.at[n], down)

    def z_detour(s, j):
        n = s * GRID + j
        k = s * (GRID // 2) + j // 2
        return remote(z_send.at[n], z_relay.at[k], z_ss.at[n], z_in.at[k], down_relay)

    def z_resend(s, j):
        n = s * GRID + j
        k = s * (GRID // 2) + j // 2
        return remote(z_relay.at[k], z_recv.at[n], z_on.at[k], z_rs.at[n], down_relay_on)

    def z_start(s, j):
        detour = wraps_down & (lax.rem(j, 2) == 1)
        pl.when(detour)(lambda: z_detour(s, j).start())
        pl.when(jnp.logical_not(detour))(lambda: z_copy(s, j).start())

    def relay_down(s, j):
        def run():
            z_detour(s, j).wait_recv()
            z_resend(s, j).start()

        pl.when(relays_down & (lax.rem(j, 2) == 1))(run)

    def z_step(s, j):
        value = term(3 - s, j)
        if s > 0:
            relay_down(s - 1, j)
            z_copy(s - 1, j).wait_recv()
            value = value + z_recv[(s - 1) * GRID + j]
        z_send[s * GRID + j] = value
        z_start(s, j)

    def f_copy(j):
        return remote(f_send.at[j], f_recv.at[j], f_ss.at[j], f_rs.at[j], mate)

    def last_step(j):
        value = term(0, j)
        relay_down(2, j)
        z_copy(2, j).wait_recv()
        value = value + z_recv[2 * GRID + j]
        parts = split(value.T)
        f_send[j] = dot3(parts, (wt_hi[other], wt_lo[other]))
        f_copy(j).start()
        f_own[j] = dot3(parts, (wt_hi[feat], wt_lo[feat]))

    scale = F32(1.0 / math.sqrt(ROWS * PARTS))

    def weight_part(source, half, c):
        grad = dot3((pgt_hi[...], pgt_lo[...]), split(source[c])).T * scale
        for h in range(2):
            start = pl.multiple_of(h * 512 + half * HALF + c * LANES, LANES)
            ar[pl.ds(start, LANES), :] = grad[:, h * LANES:(h + 1) * LANES]

    def rows_at(start, size, ref):
        return ref.at[pl.ds(pl.multiple_of(start, 8), size)]

    def read_at(start, size, ref):
        return ref[pl.ds(pl.multiple_of(start, 8), size), :]

    def sum_core():
        return remote(rows_at((1 - core) * 512, 512, ar), ar_core, ar_ss.at[0], ar_rs.at[0], core_peer)

    def sum_x(d):
        return remote(
            rows_at(x_peer(d) * 128, 128, s1), ar_x.at[d - 1], ar_ss.at[d], ar_rs.at[d],
            at(x_peer(d), y, z, core),
        )

    def sum_y():
        return remote(rows_at((1 - y) * 64, 64, s2), ar_y, ar_ss.at[4], ar_rs.at[4], y_peer)

    def sum_z(d):
        return remote(
            rows_at(z_peer(d) * 8, 8, s3), ar_z.at[d - 1], ar_ss.at[4 + d], ar_rs.at[4 + d],
            at(x, y, z_peer(d), core),
        )

    base_core = core * 512
    base_x = base_core + x * 128
    base_y = base_x + y * 64
    base_z = base_y + z * 8

    def share(base, size, n, device):
        return remote(rows_at(base, size, ag), rows_at(base, size, ag), ag_ss.at[n], ag_rs.at[n], device)

    def share_z(d):
        return share(base_z, 8, d - 1, at(x, y, z_peer(d), core))

    def share_y():
        return share(base_y, 64, 7, y_peer)

    def share_x(d):
        return share(base_x, 128, 7 + d, at(x_peer(d), y, z, core))

    def share_core():
        return share(base_core, 512, 11, core_peer)

    def landed_z(d):
        peer = lax.rem(z + Z - d, Z)
        return share(base_y + peer * 8, 8, d - 1, mate)

    def landed_y():
        return share(base_x + (1 - y) * 64, 64, 7, mate)

    def landed_x(d):
        peer = lax.rem(x + X - d, X)
        return share(base_core + peer * 128, 128, 7 + d, mate)

    def landed_core():
        return share((1 - core) * 512, 512, 11, mate)

    def point0():
        sum_core().start()

    def point1():
        sum_core().wait_recv()
        s1[...] = read_at(base_core, 512, ar) + ar_core[...]
        for d in range(1, X):
            sum_x(d).start()

    def point2():
        total = read_at(x * 128, 128, s1)
        for d in range(1, X):
            sum_x(d).wait_recv()
            total = total + ar_x[d - 1]
        s2[...] = total
        sum_y().start()

    def point3():
        sum_y().wait_recv()
        s3[...] = read_at(y * 64, 64, s2) + ar_y[...]
        for d in range(1, Z):
            sum_z(d).start()

    def point4():
        total = read_at(z * 8, 8, s3)
        for d in range(1, Z):
            sum_z(d).wait_recv()
            total = total + ar_z[d - 1]
        ag[pl.ds(pl.multiple_of(base_z, 8), 8), :] = total
        for d in range(1, Z):
            share_z(d).start()

    def point5():
        for d in range(1, Z):
            landed_z(d).wait_recv()
        share_y().start()

    def point6():
        landed_y().wait_recv()
        for d in range(1, X):
            share_x(d).start()

    def point7():
        for d in range(1, X):
            landed_x(d).wait_recv()
        share_core().start()

    wgrad_copy = pltpu.make_async_copy(wg, wgrad_out, local_sem.at[5])

    def point8():
        landed_core().wait_recv()
        for h in range(2):
            wg[:, h * LANES:(h + 1) * LANES] = ag[pl.ds(h * 512, 512), :]
        wgrad_copy.start()

    each(GRID, lambda j: z_step(0, j))
    for c in range(2):
        weight_part(agg, feat, c)
        weight_part(agg_far, other, c)
    point0()
    each(4, lambda j: z_step(1, j))
    point1()
    each(4, lambda j: z_step(1, j), 4)
    point2()
    each(4, lambda j: z_step(2, j))
    point3()
    each(4, lambda j: z_step(2, j), 4)
    point4()
    each(2, last_step)
    point5()
    each(2, last_step, 2)
    point6()
    each(2, last_step, 4)
    point7()
    each(2, last_step, 6)
    point8()

    def finish(j):
        f_copy(j).wait_recv()
        f_own[j] += f_recv[j]
        rows = pl.ds(pl.multiple_of(j * LANES, LANES), LANES)
        pltpu.make_async_copy(f_own.at[j], grad_out.at[rows], local_sem.at[6 + j]).start()

    each(GRID, finish)

    for c in range(2):
        for w in range(1, SLOTS):
            for j in range(4):
                fwd_copy(w, c, j).wait_send()
            pl.when(relays_up)(lambda w=w, c=c: [fwd_resend(w, c, j).wait_send() for j in (1, 3)] and None)
        for i in range(2):
            y_copy(c, i).wait_send()

    def sent(j):
        for s in range(3):
            z_copy(s, j).wait_send()
            pl.when(relays_down & (lax.rem(j, 2) == 1))(lambda s=s: z_resend(s, j).wait_send())
        f_copy(j).wait_send()

    each(GRID, sent)
    sum_core().wait_send()
    sum_y().wait_send()
    share_core().wait_send()
    share_y().wait_send()
    for d in range(1, X):
        sum_x(d).wait_send()
        share_x(d).wait_send()
    for d in range(1, Z):
        sum_z(d).wait_send()
        share_z(d).wait_send()
    act_copy.wait()
    wgrad_copy.wait()

    def written(j):
        rows = pl.ds(pl.multiple_of(j * LANES, LANES), LANES)
        pltpu.make_async_copy(f_own.at[j], grad_out.at[rows], local_sem.at[6 + j]).wait()

    each(GRID, written)


def copy_kernel(a_in, b_in, c_in, a_out, b_out, c_out, a, b, c, sems):
    groups = ((a_in, a, a_out), (b_in, b, b_out), (c_in, c, c_out))
    reads, writes = [], []
    for i, (src, mid, dst) in enumerate(groups):
        size = src.shape[0] // 4
        for k in range(4):
            rows = pl.ds(k * size, size)
            reads.append(pltpu.make_async_copy(src.at[rows], mid.at[rows], sems.at[i * 4 + k]))
            writes.append(pltpu.make_async_copy(mid.at[rows], dst.at[rows], sems.at[12 + i * 4 + k]))
    for read in reads:
        read.start()
    for read, write in zip(reads, writes):
        read.wait()
        write.start()
    for write in writes:
        write.wait()


def body(features, weight, cotangent, block_rows, block_cols, block_counts, block_values):
    order = jnp.arange(CAP, dtype=jnp.int32)
    live = order[None, :] < block_counts[0][:, None]
    place = jnp.where(live, block_rows[0] * GRID + block_cols[0], -1)
    hit = place[:, None, :] == jnp.arange(GRID * GRID, dtype=jnp.int32)[None, :, None]
    table = jnp.max(jnp.where(hit, order[None, None, :], -1), axis=2).reshape(-1)
    vmem = pltpu.VMEM
    dma = pltpu.SemaphoreType.DMA
    anywhere = pl.BlockSpec(memory_space=pl.ANY)
    results = pl.pallas_call(
        kernel,
        out_shape=(
            jax.ShapeDtypeStruct((ROWS, HALF), F32),
            jax.ShapeDtypeStruct((ROWS, HALF), F32),
            jax.ShapeDtypeStruct((2 * HALF, HALF), F32),
        ),
        in_specs=[pl.BlockSpec(memory_space=pltpu.SMEM)] + [anywhere] * 4,
        out_specs=(anywhere,) * 3,
        scratch_shapes=[
            vmem((SLOTS * CAP, LANES, LANES), F32),
            vmem((SLOTS * GRID, ROWS, LANES), BF16),
            vmem((SLOTS * GRID, ROWS, LANES), BF16),
            vmem((ROWS, HALF), F32),
            vmem((2 * HALF, HALF), F32),
            vmem((2, HALF, HALF), BF16),
            vmem((2, HALF, HALF), BF16),
            vmem((2, HALF, HALF), BF16),
            vmem((2, HALF, HALF), BF16),
            vmem((ROWS, HALF), F32),
            vmem((24, 256, LANES), F32),
            vmem((2, ROWS, LANES), F32),
            vmem((2, ROWS, LANES), F32),
            vmem((ROWS, HALF), F32),
            vmem((ROWS, HALF), F32),
            vmem((HALF, ROWS), BF16),
            vmem((HALF, ROWS), BF16),
            vmem((3 * GRID, HALF, LANES), F32),
            vmem((3 * GRID, HALF, LANES), F32),
            vmem((GRID, LANES, HALF), F32),
            vmem((GRID, LANES, HALF), F32),
            vmem((GRID, LANES, HALF), F32),
            vmem((1024, LANES), F32),
            vmem((512, LANES), F32),
            vmem((512, LANES), F32),
            vmem((3, 128, LANES), F32),
            vmem((128, LANES), F32),
            vmem((64, LANES), F32),
            vmem((64, LANES), F32),
            vmem((7, 8, LANES), F32),
            vmem((1024, LANES), F32),
            vmem((2 * HALF, HALF), F32),
            vmem((12, 256, LANES), F32),
            vmem((12, HALF, LANES), F32),
            dma((14,)),
            dma((24,)), dma((24,)),
            dma((4,)), dma((4,)),
            dma((24,)), dma((24,)),
            dma((8,)), dma((8,)),
            dma((12,)), dma((12,)), dma((12,)), dma((12,)),
            dma((12,)), dma((12,)),
            dma((12,)), dma((12,)),
        ],
        compiler_params=pltpu.CompilerParams(
            collective_id=0, has_side_effects=True, vmem_limit_bytes=56 * 2**20
        ),
        cost_estimate=pl.CostEstimate(flops=16 * 10**9, bytes_accessed=12 * 2**20, transcendentals=ROWS * HALF),
        name="layer",
    )(table, features, weight, cotangent, block_values.reshape(SLOTS * CAP, LANES, LANES))
    return pl.pallas_call(
        copy_kernel,
        out_shape=tuple(jax.ShapeDtypeStruct(r.shape, F32) for r in results),
        in_specs=[anywhere] * 3,
        out_specs=(anywhere,) * 3,
        scratch_shapes=[vmem(r.shape, F32) for r in results] + [dma((24,))],
        name="results",
    )(*results)


def solution(mesh):
    in_specs = (
        P("dom", "feat"),
        P(None, "feat"),
        P("dom", "feat"),
        P("dom", None, None),
        P("dom", None, None),
        P("dom", None),
        P("dom", None, None, None, None),
    )
    out_specs = (P("dom", "feat"), P("dom", "feat"), P(None, "feat"))
    return jax.shard_map(body, mesh=mesh, in_specs=in_specs, out_specs=out_specs, check_vma=False)
```

```python
import math

import jax
import jax.numpy as jnp
from jax import lax
from jax.experimental import pallas as pl
from jax.experimental.pallas import tpu as pltpu
from jax.sharding import PartitionSpec as P

MESH = pl.DeviceIdType.MESH
F32 = jnp.float32
BF16 = jnp.bfloat16
X, Y, Z, CORES = 4, 2, 8, 2
PARTS = X * Y * Z * CORES
SLOTS, CAP, GRID = 4, 24, 8
ROWS, HALF, LANES = 1024, 256, 128


def split(value):
    high = value.astype(BF16)
    return high, (value - high.astype(F32)).astype(BF16)


def dot(a, b):
    return jnp.dot(a, b, preferred_element_type=F32)


def dot3(a, b):
    return dot(a[0], b[0]) + dot(a[1], b[0]) + dot(a[0], b[1])


def remote(src, dst, send, recv, device):
    return pltpu.make_async_remote_copy(
        src_ref=src, dst_ref=dst, send_sem=send, recv_sem=recv,
        device_id=device, device_id_type=MESH,
    )


def kernel(
    table, features, weight, cotangent, blocks_in,
    act_out, grad_out, wgrad_out,
    blocks, adj_hi, adj_lo, own, w_raw, w_hi, w_lo, wt_hi, wt_lo, cot,
    fwd, side_hi, side_lo, agg, agg_far, pre, act, pgt,
    z_send, z_recv, f_send, f_recv, f_own,
    ar, ar_core, s1, ar_x, s2, ar_y, s3, ar_z, ag,
    fwd_relay, z_relay,
    local_sem, fwd_ss, fwd_rs, y_ss, y_rs, z_ss, z_rs, f_ss, f_rs,
    fwd_in, fwd_on, z_in, z_on,
    ar_ss, ar_rs, ag_ss, ag_rs,
):
    me = lax.axis_index("dom")
    feat = lax.axis_index("feat")
    other = 1 - feat
    core = lax.rem(me, 2)
    z = lax.rem(me // 2, Z)
    y = lax.rem(me // (2 * Z), Y)
    x = me // (2 * Z * Y)
    up = (lax.rem(me + 1, PARTS), feat)
    down = (lax.rem(me + PARTS - 1, PARTS), feat)
    mate = (me, other)

    def at(x_, y_, z_, core_):
        return (((x_ * Y + y_) * Z + z_) * 2 + core_, feat)

    core_peer = at(x, y, z, 1 - core)
    x_next, x_before = lax.rem(x + y, X), lax.rem(x + y + X - 1, X)
    first_z, last_z = z == 0, z == Z - 1
    is_odd, is_even = core == 1, core == 0
    wraps_up, wraps_down = is_odd & last_z, is_even & first_z
    relays_up, relays_down = is_even & last_z, is_odd & first_z
    up_relay = at(x_next, 1 - y, Z - 1, 0)
    up_relay_on = at(x, y, 0, 0)
    down_relay = at(x_before, 1 - y, 0, 1)
    down_relay_on = at(x, y, Z - 1, 1)
    y_peer = at(x, 1 - y, z, core)

    def x_peer(d):
        return lax.rem(x + d, X)

    def z_peer(d):
        return lax.rem(z + d, Z)

    loads = [
        pltpu.make_async_copy(blocks_in, blocks, local_sem.at[0]),
        pltpu.make_async_copy(features, own, local_sem.at[1]),
        pltpu.make_async_copy(weight, w_raw, local_sem.at[2]),
        pltpu.make_async_copy(cotangent, cot, local_sem.at[3]),
    ]
    for load in loads:
        load.start()

    barrier = pltpu.get_barrier_semaphore()
    partners = [up, down, mate, y_peer]
    partners += [at(x_peer(d), y, z, core) for d in range(1, X)]
    partners += [at(x, y, z_peer(d), core) for d in range(1, Z)]
    partners += [at(x_next, 1 - y, z, 1 - core), at(x_before, 1 - y, z, 1 - core)]
    for partner in partners:
        pl.semaphore_signal(barrier, inc=1, device_id=partner, device_id_type=MESH)
    pl.semaphore_wait(barrier, len(partners))

    def fwd_at(w, c, j):
        return ((w - 1) * 2 + c) * 4 + j

    def fwd_copy(w, c, j):
        i = fwd_at(w, c, j)
        if w == 1:
            src = features.at[pl.ds(j * 256, 256), pl.ds(c * LANES, LANES)]
        else:
            src = fwd.at[fwd_at(w - 1, c, j)]
        return remote(src, fwd.at[i], fwd_ss.at[i], fwd_rs.at[i], up)

    def fwd_detour(w, c, j):
        i = fwd_at(w, c, j)
        if w == 1:
            src = features.at[pl.ds(j * 256, 256), pl.ds(c * LANES, LANES)]
        else:
            src = fwd.at[fwd_at(w - 1, c, j)]
        n = fwd_at(w, c, 0) // 2 + j // 2
        return remote(src, fwd_relay.at[n], fwd_ss.at[i], fwd_in.at[n], up_relay)

    def fwd_resend(w, c, j):
        i = fwd_at(w, c, j)
        n = fwd_at(w, c, 0) // 2 + j // 2
        return remote(fwd_relay.at[n], fwd.at[i], fwd_on.at[n], fwd_rs.at[i], up_relay_on)

    def fwd_start(w, c, j):
        if j % 2 == 0:
            fwd_copy(w, c, j).start()
        else:
            pl.when(wraps_up)(lambda: fwd_detour(w, c, j).start())
            pl.when(jnp.logical_not(wraps_up))(lambda: fwd_copy(w, c, j).start())

    def relay_up(w, c):
        def run():
            for j in (1, 3):
                fwd_detour(w, c, j).wait_recv()
                fwd_resend(w, c, j).start()

        pl.when(relays_up)(run)

    def each(n, body, start=0):
        def step(j, carry):
            body(j)
            return carry

        lax.fori_loop(start, start + n, step, 0)

    def send_own(c):
        for j in range(4):
            fwd_start(1, c, j)

    def pass_on(w, c):
        for j in range(4):
            fwd_copy(w, c, j).wait_recv()
            fwd_start(w + 1, c, j)

    def densify(w):
        def body(r):
            rows = pl.ds(pl.multiple_of(r * LANES, LANES), LANES)
            for c in range(GRID):
                found = table[(w * GRID + r) * GRID + c]
                live = jnp.where(found >= 0, 1.0, 0.0).astype(F32)
                high, low = split(blocks[w * CAP + jnp.maximum(found, 0)] * live)
                adj_hi[w * GRID + c, rows, :] = high
                adj_lo[w * GRID + c, rows, :] = low

        each(GRID, body)

    def gather_in(w, c, j, piece, last=None):
        high, low = split(piece)
        both = jnp.concatenate([high, low], axis=1)

        def body(i):
            rows = pl.ds(pl.multiple_of(i * 512, 512), 512)
            a_hi = jnp.concatenate(
                [adj_hi[w * GRID + 2 * j, rows, :], adj_hi[w * GRID + 2 * j + 1, rows, :]], axis=1
            )
            a_lo = jnp.concatenate(
                [adj_lo[w * GRID + 2 * j, rows, :], adj_lo[w * GRID + 2 * j + 1, rows, :]], axis=1
            )
            wide = dot(a_hi, both)
            total = wide[:, :LANES] + wide[:, LANES:] + dot(a_lo, high)
            agg[c, rows, :] += total
            if last is not None:
                last(i)

        each(2, body)

    def tile(adj, w, i):
        rows = pl.ds(pl.multiple_of(i * 256, 256), 256)
        return jnp.concatenate([adj[w * GRID + k, rows, :] for k in range(GRID)], axis=1)

    def gather_own():
        for c in range(2):
            high, low = split(own[:, c * LANES:(c + 1) * LANES])
            side_hi[:, c * LANES:(c + 1) * LANES] = high
            side_lo[:, c * LANES:(c + 1) * LANES] = low

        def body(i):
            a_hi, a_lo = tile(adj_hi, 0, i), tile(adj_lo, 0, i)
            total = dot(a_hi, side_hi[...]) + dot(a_hi, side_lo[...]) + dot(a_lo, side_hi[...])
            rows = pl.ds(pl.multiple_of(i * 256, 256), 256)
            for c in range(2):
                agg[c, rows, :] = total[:, c * LANES:(c + 1) * LANES]

        each(4, body)

    def gather_slot(w, c):
        for j in range(4):
            high, low = split(fwd[fwd_at(w, c, j)])
            side_hi[j * 256:(j + 1) * 256, :LANES] = high
            side_hi[j * 256:(j + 1) * 256, LANES:] = low

        def body(i):
            wide = dot(tile(adj_hi, w, i), side_hi[...])
            rest = dot(tile(adj_lo, w, i), side_hi[:, :LANES])
            rows = pl.ds(pl.multiple_of(i * 256, 256), 256)
            agg[c, rows, :] += wide[:, :LANES] + wide[:, LANES:] + rest

        each(4, body)

    def y_copy(c, i):
        rows = pl.ds(pl.multiple_of(i * 256, 256), 256)
        n = c * 4 + i
        return remote(agg.at[c, rows], agg_far.at[c, rows], y_ss.at[n], y_rs.at[n], mate)

    def y_start(c, i):
        y_copy(c, 2 * i).start()
        y_copy(c, 2 * i + 1).start()

    def gather_last(c):
        def body(j):
            fwd_copy(3, c, j).wait_recv()
            gather_in(3, c, j, fwd[fwd_at(3, c, j)])

        each(3, body)
        fwd_copy(3, c, 3).wait_recv()
        gather_in(3, c, 3, fwd[fwd_at(3, c, 3)], last=lambda i: y_start(c, i))

    send_own(0)
    loads[0].wait()
    densify(0)
    densify(1)
    relay_up(1, 0)
    pass_on(1, 0)
    send_own(1)
    densify(2)
    densify(3)
    relay_up(2, 0)
    pass_on(2, 0)
    relay_up(3, 0)
    loads[1].wait()
    gather_own()
    gather_slot(1, 0)
    relay_up(1, 1)
    gather_slot(2, 0)
    gather_last(0)
    relay_up(2, 1)
    pass_on(1, 1)
    gather_slot(1, 1)
    relay_up(3, 1)
    pass_on(2, 1)
    gather_slot(2, 1)

    loads[2].wait()
    for k in range(2):
        value = w_raw[pl.ds(k * HALF, HALF), :]
        w_hi[k], w_lo[k] = split(value)
        wt_hi[k], wt_lo[k] = split(value.T)
    loads[3].wait()
    gather_last(1)

    def near_part(i):
        rows = pl.ds(pl.multiple_of(i * 256, 256), 256)
        value = jnp.concatenate([agg[0, rows, :], agg[1, rows, :]], axis=1)
        pre[rows, :] = dot3(split(value), (w_hi[feat], w_lo[feat]))

    each(4, near_part)
    for i in range(4):
        y_copy(0, i).wait_recv()

    def far_part(c, i):
        rows = pl.ds(pl.multiple_of(i * 256, 256), 256)
        ks = pl.ds(c * LANES, LANES)
        return dot3(split(agg_far[c, rows, :]), (w_hi[other, ks, :], w_lo[other, ks, :]))

    def far_first(i):
        rows = pl.ds(pl.multiple_of(i * 256, 256), 256)
        pre[rows, :] += far_part(0, i)

    each(4, far_first)

    def activate(i):
        rows = pl.ds(pl.multiple_of(i * 256, 256), 256)
        y_copy(1, i).wait_recv()
        value = pre[rows, :] + far_part(1, i)
        s = jax.nn.sigmoid(value)
        act[rows, :] = value * s
        grad = cot[rows, :] * (s + value * s * (1.0 - s))
        pgt[:HALF, rows], pgt[HALF:, rows] = split(grad.T)

    each(4, activate)
    act_copy = pltpu.make_async_copy(act, act_out, local_sem.at[4])
    act_copy.start()

    def times_pgt(high, low):
        both = dot(pgt[...], high)
        return both[:HALF] + both[HALF:] + dot(pgt[:HALF, :], low)

    def term(w, j, count):
        n = w * GRID + j
        if count == 1:
            return times_pgt(adj_hi[n], adj_lo[n])
        return times_pgt(
            jnp.concatenate([adj_hi[n], adj_hi[n + 1]], axis=1),
            jnp.concatenate([adj_lo[n], adj_lo[n + 1]], axis=1),
        )

    def z_copy(s, j):
        n = s * GRID + j
        return remote(z_send.at[n], z_recv.at[n], z_ss.at[n], z_rs.at[n], down)

    def z_detour(s, j):
        n = s * GRID + j
        k = s * (GRID // 2) + j // 2
        return remote(z_send.at[n], z_relay.at[k], z_ss.at[n], z_in.at[k], down_relay)

    def z_resend(s, j):
        n = s * GRID + j
        k = s * (GRID // 2) + j // 2
        return remote(z_relay.at[k], z_recv.at[n], z_on.at[k], z_rs.at[n], down_relay_on)

    def z_start(s, j, odd):
        if odd:
            pl.when(wraps_down)(lambda: z_detour(s, j).start())
            pl.when(jnp.logical_not(wraps_down))(lambda: z_copy(s, j).start())
        else:
            z_copy(s, j).start()

    def carried(s, j, odd):
        if odd:
            def run():
                z_detour(s, j).wait_recv()
                z_resend(s, j).start()

            pl.when(relays_down)(run)
        z_copy(s, j).wait_recv()
        return z_recv[s * GRID + j]

    def z_step(s, pair):
        value = term(3 - s, 2 * pair, 2)
        for h in range(2):
            j = 2 * pair + h
            part = value[:, h * LANES:(h + 1) * LANES]
            if s > 0:
                part = part + carried(s - 1, j, h == 1)
            z_send[s * GRID + j] = part
            z_start(s, j, h == 1)

    def f_copy(j):
        return remote(f_send.at[j], f_recv.at[j], f_ss.at[j], f_rs.at[j], mate)

    def last_step(start, odds):
        count = len(odds)
        value = term(0, start, count)
        sums = [
            value[:, h * LANES:(h + 1) * LANES] + carried(2, start + h, odd)
            for h, odd in enumerate(odds)
        ]
        parts = split(jnp.concatenate(sums, axis=1).T)
        far = dot3(parts, (wt_hi[other], wt_lo[other]))
        for h in range(count):
            f_send[start + h] = far[h * LANES:(h + 1) * LANES]
            f_copy(start + h).start()
        near = dot3(parts, (wt_hi[feat], wt_lo[feat]))
        for h in range(count):
            f_own[start + h] = near[h * LANES:(h + 1) * LANES]

    scale = F32(1.0 / math.sqrt(ROWS * PARTS))

    def weight_part(source, half):
        high, low = split(jnp.concatenate([source[0], source[1]], axis=1))
        grad = times_pgt(high, low).T * scale
        for h in range(2):
            start = pl.multiple_of(h * 512 + half * HALF, HALF)
            ar[pl.ds(start, HALF), :] = grad[:, h * LANES:(h + 1) * LANES]

    def rows_at(start, size, ref):
        return ref.at[pl.ds(pl.multiple_of(start, 8), size)]

    def read_at(start, size, ref):
        return ref[pl.ds(pl.multiple_of(start, 8), size), :]

    def sum_core():
        return remote(rows_at((1 - core) * 512, 512, ar), ar_core, ar_ss.at[0], ar_rs.at[0], core_peer)

    def sum_x(d):
        return remote(
            rows_at(x_peer(d) * 128, 128, s1), ar_x.at[d - 1], ar_ss.at[d], ar_rs.at[d],
            at(x_peer(d), y, z, core),
        )

    def sum_y():
        return remote(rows_at((1 - y) * 64, 64, s2), ar_y, ar_ss.at[4], ar_rs.at[4], y_peer)

    def sum_z(d):
        return remote(
            rows_at(z_peer(d) * 8, 8, s3), ar_z.at[d - 1], ar_ss.at[4 + d], ar_rs.at[4 + d],
            at(x, y, z_peer(d), core),
        )

    base_core = core * 512
    base_x = base_core + x * 128
    base_y = base_x + y * 64
    base_z = base_y + z * 8

    def share(base, size, n, device):
        return remote(rows_at(base, size, ag), rows_at(base, size, ag), ag_ss.at[n], ag_rs.at[n], device)

    def share_z(d):
        return share(base_z, 8, d - 1, at(x, y, z_peer(d), core))

    def share_y():
        return share(base_y, 64, 7, y_peer)

    def share_x(d):
        return share(base_x, 128, 7 + d, at(x_peer(d), y, z, core))

    def share_core():
        return share(base_core, 512, 11, core_peer)

    def landed_z(d):
        peer = lax.rem(z + Z - d, Z)
        return share(base_y + peer * 8, 8, d - 1, mate)

    def landed_y():
        return share(base_x + (1 - y) * 64, 64, 7, mate)

    def landed_x(d):
        peer = lax.rem(x + X - d, X)
        return share(base_core + peer * 128, 128, 7 + d, mate)

    def landed_core():
        return share((1 - core) * 512, 512, 11, mate)

    def point0():
        sum_core().start()

    def point1():
        sum_core().wait_recv()
        s1[...] = read_at(base_core, 512, ar) + ar_core[...]
        for d in range(1, X):
            sum_x(d).start()

    def point2():
        total = read_at(x * 128, 128, s1)
        for d in range(1, X):
            sum_x(d).wait_recv()
            total = total + ar_x[d - 1]
        s2[...] = total
        sum_y().start()

    def point3():
        sum_y().wait_recv()
        s3[...] = read_at(y * 64, 64, s2) + ar_y[...]
        for d in range(1, Z):
            sum_z(d).start()

    def point4():
        total = read_at(z * 8, 8, s3)
        for d in range(1, Z):
            sum_z(d).wait_recv()
            total = total + ar_z[d - 1]
        ag[pl.ds(pl.multiple_of(base_z, 8), 8), :] = total
        for d in range(1, Z):
            share_z(d).start()

    def point5():
        for d in range(1, Z):
            landed_z(d).wait_recv()
        share_y().start()

    def point6():
        landed_y().wait_recv()
        for d in range(1, X):
            share_x(d).start()

    def point7():
        for d in range(1, X):
            landed_x(d).wait_recv()
        share_core().start()

    wgrad_copies = [
        pltpu.make_async_copy(
            ag.at[pl.ds(h * 512, 512)], wgrad_out.at[:, pl.ds(h * LANES, LANES)], local_sem.at[(5, 14)[h]]
        )
        for h in range(2)
    ]

    def point8():
        landed_core().wait_recv()
        for copy in wgrad_copies:
            copy.start()

    late = first_z | (z >= Z - 2)
    soon = jnp.logical_not(late)

    def after(i, points, where):
        for k, point in points.items():
            pl.when((i == k) & where)(point)

    def third(i):
        z_step(2, i)
        after(i, {2: point4, 3: point5}, is_odd & late)
        after(i, {3: point4}, is_even & late)

    def fourth(i):
        last_step(2 * i, (False, True))
        after(i, {0: point6, 1: point7}, is_odd & late)
        after(i, {0: point5, 1: point6, 2: point7}, is_even & late)
        after(i, {0: point4, 1: point5, 2: point6}, is_odd & soon)

    def even_end():
        point4()
        point5()
        point6()

    each(4, lambda i: z_step(0, i))
    weight_part(agg, feat)
    weight_part(agg_far, other)
    point0()
    point1()
    point2()
    each(4, lambda i: z_step(1, i))
    point3()
    each(4, third)
    each(3, fourth)
    last_step(6, (False,))
    last_step(7, (True,))
    pl.when(is_even & soon)(even_end)
    pl.when(soon)(point7)

    def finish(j):
        f_copy(j).wait_recv()
        f_own[j] += f_recv[j]
        rows = pl.ds(pl.multiple_of(j * LANES, LANES), LANES)
        pltpu.make_async_copy(f_own.at[j], grad_out.at[rows], local_sem.at[6 + j]).start()

    each(GRID, finish)
    point8()

    for c in range(2):
        for w in range(1, SLOTS):
            for j in range(4):
                fwd_copy(w, c, j).wait_send()
            pl.when(relays_up)(lambda w=w, c=c: [fwd_resend(w, c, j).wait_send() for j in (1, 3)] and None)
        for i in range(4):
            y_copy(c, i).wait_send()

    def sent(j):
        for s in range(3):
            z_copy(s, j).wait_send()
            pl.when(relays_down & (lax.rem(j, 2) == 1))(lambda s=s: z_resend(s, j).wait_send())
        f_copy(j).wait_send()

    each(GRID, sent)
    sum_core().wait_send()
    sum_y().wait_send()
    share_core().wait_send()
    share_y().wait_send()
    for d in range(1, X):
        sum_x(d).wait_send()
        share_x(d).wait_send()
    for d in range(1, Z):
        sum_z(d).wait_send()
        share_z(d).wait_send()
    act_copy.wait()
    for copy in wgrad_copies:
        copy.wait()

    def written(j):
        rows = pl.ds(pl.multiple_of(j * LANES, LANES), LANES)
        pltpu.make_async_copy(f_own.at[j], grad_out.at[rows], local_sem.at[6 + j]).wait()

    each(GRID, written)


def copy_kernel(a_in, b_in, c_in, a_out, b_out, c_out, a, b, c, sems):
    groups = ((a_in, a, a_out), (b_in, b, b_out), (c_in, c, c_out))
    reads, writes = [], []
    for i, (src, mid, dst) in enumerate(groups):
        size = src.shape[0] // 4
        for k in range(4):
            rows = pl.ds(k * size, size)
            reads.append(pltpu.make_async_copy(src.at[rows], mid.at[rows], sems.at[i * 4 + k]))
            writes.append(pltpu.make_async_copy(mid.at[rows], dst.at[rows], sems.at[12 + i * 4 + k]))
    for read in reads:
        read.start()
    for read, write in zip(reads, writes):
        read.wait()
        write.start()
    for write in writes:
        write.wait()


def body(features, weight, cotangent, block_rows, block_cols, block_counts, block_values):
    order = jnp.arange(CAP, dtype=jnp.int32)
    live = order[None, :] < block_counts[0][:, None]
    place = jnp.where(live, block_rows[0] * GRID + block_cols[0], -1)
    hit = place[:, None, :] == jnp.arange(GRID * GRID, dtype=jnp.int32)[None, :, None]
    table = jnp.max(jnp.where(hit, order[None, None, :], -1), axis=2).reshape(-1)
    vmem = pltpu.VMEM
    dma = pltpu.SemaphoreType.DMA
    anywhere = pl.BlockSpec(memory_space=pl.ANY)
    results = pl.pallas_call(
        kernel,
        out_shape=(
            jax.ShapeDtypeStruct((ROWS, HALF), F32),
            jax.ShapeDtypeStruct((ROWS, HALF), F32),
            jax.ShapeDtypeStruct((2 * HALF, HALF), F32),
        ),
        in_specs=[pl.BlockSpec(memory_space=pltpu.SMEM)] + [anywhere] * 4,
        out_specs=(anywhere,) * 3,
        scratch_shapes=[
            vmem((SLOTS * CAP, LANES, LANES), F32),
            vmem((SLOTS * GRID, ROWS, LANES), BF16),
            vmem((SLOTS * GRID, ROWS, LANES), BF16),
            vmem((ROWS, HALF), F32),
            vmem((2 * HALF, HALF), F32),
            vmem((2, HALF, HALF), BF16),
            vmem((2, HALF, HALF), BF16),
            vmem((2, HALF, HALF), BF16),
            vmem((2, HALF, HALF), BF16),
            vmem((ROWS, HALF), F32),
            vmem((24, 256, LANES), F32),
            vmem((ROWS, HALF), BF16),
            vmem((ROWS, HALF), BF16),
            vmem((2, ROWS, LANES), F32),
            vmem((2, ROWS, LANES), F32),
            vmem((ROWS, HALF), F32),
            vmem((ROWS, HALF), F32),
            vmem((2 * HALF, ROWS), BF16),
            vmem((3 * GRID, HALF, LANES), F32),
            vmem((3 * GRID, HALF, LANES), F32),
            vmem((GRID, LANES, HALF), F32),
            vmem((GRID, LANES, HALF), F32),
            vmem((GRID, LANES, HALF), F32),
            vmem((1024, LANES), F32),
            vmem((512, LANES), F32),
            vmem((512, LANES), F32),
            vmem((3, 128, LANES), F32),
            vmem((128, LANES), F32),
            vmem((64, LANES), F32),
            vmem((64, LANES), F32),
            vmem((7, 8, LANES), F32),
            vmem((1024, LANES), F32),
            vmem((12, 256, LANES), F32),
            vmem((12, HALF, LANES), F32),
            dma((15,)),
            dma((24,)), dma((24,)),
            dma((8,)), dma((8,)),
            dma((24,)), dma((24,)),
            dma((8,)), dma((8,)),
            dma((12,)), dma((12,)), dma((12,)), dma((12,)),
            dma((12,)), dma((12,)),
            dma((12,)), dma((12,)),
        ],
        compiler_params=pltpu.CompilerParams(
            collective_id=0, has_side_effects=True, vmem_limit_bytes=56 * 2**20
        ),
        cost_estimate=pl.CostEstimate(flops=16 * 10**9, bytes_accessed=12 * 2**20, transcendentals=ROWS * HALF),
        name="layer",
    )(table, features, weight, cotangent, block_values.reshape(SLOTS * CAP, LANES, LANES))
    return pl.pallas_call(
        copy_kernel,
        out_shape=tuple(jax.ShapeDtypeStruct(r.shape, F32) for r in results),
        in_specs=[anywhere] * 3,
        out_specs=(anywhere,) * 3,
        scratch_shapes=[vmem(r.shape, F32) for r in results] + [dma((24,))],
        name="results",
    )(*results)


def solution(mesh):
    in_specs = (
        P("dom", "feat"),
        P(None, "feat"),
        P("dom", "feat"),
        P("dom", None, None),
        P("dom", None, None),
        P("dom", None),
        P("dom", None, None, None, None),
    )
    out_specs = (P("dom", "feat"), P("dom", "feat"), P(None, "feat"))
    return jax.shard_map(body, mesh=mesh, in_specs=in_specs, out_specs=out_specs, check_vma=False)
```

```python
import math

import jax
import jax.numpy as jnp
from jax import lax
from jax.experimental import pallas as pl
from jax.experimental.pallas import tpu as pltpu
from jax.sharding import PartitionSpec as P

MESH = pl.DeviceIdType.MESH
F32 = jnp.float32
BF16 = jnp.bfloat16
X, Y, Z, CORES = 4, 2, 8, 2
PARTS = X * Y * Z * CORES
SLOTS, CAP, GRID = 4, 24, 8
ROWS, HALF, LANES = 1024, 256, 128


def split(value):
    high = value.astype(BF16)
    return high, (value - high.astype(F32)).astype(BF16)


def dot(a, b):
    return jnp.dot(a, b, preferred_element_type=F32)


def dot3(a, b):
    return dot(a[0], b[0]) + dot(a[1], b[0]) + dot(a[0], b[1])


def remote(src, dst, send, recv, device):
    return pltpu.make_async_remote_copy(
        src_ref=src, dst_ref=dst, send_sem=send, recv_sem=recv,
        device_id=device, device_id_type=MESH,
    )


def kernel(
    table, features, weight, cotangent, blocks_in,
    act_out, grad_out, wgrad_out,
    blocks, adj_hi, adj_lo, own, w_raw, w_hi, w_lo, wt_hi, wt_lo, cot,
    fwd, side_hi, side_lo, agg, agg_far, pre, act, pgt,
    z_send, z_recv, f_send, f_recv, f_own,
    ar, ar_core, s1, ar_x, s2, ar_y, s3, ar_z, ag,
    fwd_relay, z_relay,
    local_sem, fwd_ss, fwd_rs, y_ss, y_rs, z_ss, z_rs, f_ss, f_rs,
    fwd_in, fwd_on, z_in, z_on,
    ar_ss, ar_rs, ag_ss, ag_rs,
):
    me = lax.axis_index("dom")
    feat = lax.axis_index("feat")
    other = 1 - feat
    core = lax.rem(me, 2)
    z = lax.rem(me // 2, Z)
    y = lax.rem(me // (2 * Z), Y)
    x = me // (2 * Z * Y)
    up = (lax.rem(me + 1, PARTS), feat)
    down = (lax.rem(me + PARTS - 1, PARTS), feat)
    mate = (me, other)

    def at(x_, y_, z_, core_):
        return (((x_ * Y + y_) * Z + z_) * 2 + core_, feat)

    core_peer = at(x, y, z, 1 - core)
    x_next, x_before = lax.rem(x + y, X), lax.rem(x + y + X - 1, X)
    first_z, last_z = z == 0, z == Z - 1
    is_odd, is_even = core == 1, core == 0
    wraps_up, wraps_down = is_odd & last_z, is_even & first_z
    relays_up, relays_down = is_even & last_z, is_odd & first_z
    up_relay = at(x_next, 1 - y, Z - 1, 0)
    up_relay_on = at(x, y, 0, 0)
    down_relay = at(x_before, 1 - y, 0, 1)
    down_relay_on = at(x, y, Z - 1, 1)
    y_peer = at(x, 1 - y, z, core)

    def x_peer(d):
        return lax.rem(x + d, X)

    def z_peer(d):
        return lax.rem(z + d, Z)

    loads = [
        pltpu.make_async_copy(blocks_in, blocks, local_sem.at[0]),
        pltpu.make_async_copy(features, own, local_sem.at[1]),
        pltpu.make_async_copy(weight, w_raw, local_sem.at[2]),
        pltpu.make_async_copy(cotangent, cot, local_sem.at[3]),
    ]
    for load in loads:
        load.start()

    barrier = pltpu.get_barrier_semaphore()
    partners = [up, down, mate, y_peer]
    partners += [at(x_peer(d), y, z, core) for d in range(1, X)]
    partners += [at(x, y, z_peer(d), core) for d in range(1, Z)]
    partners += [at(x_next, 1 - y, z, 1 - core), at(x_before, 1 - y, z, 1 - core)]
    for partner in partners:
        pl.semaphore_signal(barrier, inc=1, device_id=partner, device_id_type=MESH)
    pl.semaphore_wait(barrier, len(partners))

    def fwd_at(w, c, j):
        return ((w - 1) * 2 + c) * 4 + j

    def fwd_copy(w, c, j):
        i = fwd_at(w, c, j)
        if w == 1:
            src = features.at[pl.ds(j * 256, 256), pl.ds(c * LANES, LANES)]
        else:
            src = fwd.at[fwd_at(w - 1, c, j)]
        return remote(src, fwd.at[i], fwd_ss.at[i], fwd_rs.at[i], up)

    def fwd_detour(w, c, j):
        i = fwd_at(w, c, j)
        if w == 1:
            src = features.at[pl.ds(j * 256, 256), pl.ds(c * LANES, LANES)]
        else:
            src = fwd.at[fwd_at(w - 1, c, j)]
        n = fwd_at(w, c, 0) // 2 + j // 2
        return remote(src, fwd_relay.at[n], fwd_ss.at[i], fwd_in.at[n], up_relay)

    def fwd_resend(w, c, j):
        i = fwd_at(w, c, j)
        n = fwd_at(w, c, 0) // 2 + j // 2
        return remote(fwd_relay.at[n], fwd.at[i], fwd_on.at[n], fwd_rs.at[i], up_relay_on)

    def fwd_start(w, c, j):
        if j % 2 == 0:
            fwd_copy(w, c, j).start()
        else:
            pl.when(wraps_up)(lambda: fwd_detour(w, c, j).start())
            pl.when(jnp.logical_not(wraps_up))(lambda: fwd_copy(w, c, j).start())

    def relay_up(w, c):
        def run():
            for j in (1, 3):
                fwd_detour(w, c, j).wait_recv()
                fwd_resend(w, c, j).start()

        pl.when(relays_up)(run)

    def each(n, body, start=0):
        def step(j, carry):
            body(j)
            return carry

        lax.fori_loop(start, start + n, step, 0)

    def send_own(c):
        for j in range(4):
            fwd_start(1, c, j)

    def pass_on(w, c):
        for j in range(4):
            fwd_copy(w, c, j).wait_recv()
            fwd_start(w + 1, c, j)

    def densify(w):
        def body(r):
            rows = pl.ds(pl.multiple_of(r * LANES, LANES), LANES)
            for c in range(GRID):
                found = table[(w * GRID + r) * GRID + c]
                live = jnp.where(found >= 0, 1.0, 0.0).astype(F32)
                high, low = split(blocks[w * CAP + jnp.maximum(found, 0)] * live)
                adj_hi[w * GRID + c, rows, :] = high
                adj_lo[w * GRID + c, rows, :] = low

        each(GRID, body)

    def gather_in(w, c, j, piece, last=None):
        high, low = split(piece)
        both = jnp.concatenate([high, low], axis=1)

        def body(i):
            rows = pl.ds(pl.multiple_of(i * 512, 512), 512)
            a_hi = jnp.concatenate(
                [adj_hi[w * GRID + 2 * j, rows, :], adj_hi[w * GRID + 2 * j + 1, rows, :]], axis=1
            )
            a_lo = jnp.concatenate(
                [adj_lo[w * GRID + 2 * j, rows, :], adj_lo[w * GRID + 2 * j + 1, rows, :]], axis=1
            )
            wide = dot(a_hi, both)
            total = wide[:, :LANES] + wide[:, LANES:] + dot(a_lo, high)
            agg[c, rows, :] += total
            if last is not None:
                last(i)

        each(2, body)

    def tile(adj, w, i):
        rows = pl.ds(pl.multiple_of(i * 256, 256), 256)
        return jnp.concatenate([adj[w * GRID + k, rows, :] for k in range(GRID)], axis=1)

    def gather_own():
        for c in range(2):
            high, low = split(own[:, c * LANES:(c + 1) * LANES])
            side_hi[:, c * LANES:(c + 1) * LANES] = high
            side_lo[:, c * LANES:(c + 1) * LANES] = low

        def body(i):
            a_hi, a_lo = tile(adj_hi, 0, i), tile(adj_lo, 0, i)
            total = dot(a_hi, side_hi[...]) + dot(a_hi, side_lo[...]) + dot(a_lo, side_hi[...])
            rows = pl.ds(pl.multiple_of(i * 256, 256), 256)
            for c in range(2):
                agg[c, rows, :] = total[:, c * LANES:(c + 1) * LANES]

        each(4, body)

    def gather_slot(w, c):
        for j in range(4):
            high, low = split(fwd[fwd_at(w, c, j)])
            side_hi[j * 256:(j + 1) * 256, :LANES] = high
            side_hi[j * 256:(j + 1) * 256, LANES:] = low

        def body(i):
            wide = dot(tile(adj_hi, w, i), side_hi[...])
            rest = dot(tile(adj_lo, w, i), side_hi[:, :LANES])
            rows = pl.ds(pl.multiple_of(i * 256, 256), 256)
            agg[c, rows, :] += wide[:, :LANES] + wide[:, LANES:] + rest

        each(4, body)

    def y_copy(c, i):
        rows = pl.ds(pl.multiple_of(i * 256, 256), 256)
        n = c * 4 + i
        return remote(agg.at[c, rows], agg_far.at[c, rows], y_ss.at[n], y_rs.at[n], mate)

    def y_start(c, i):
        y_copy(c, 2 * i).start()
        y_copy(c, 2 * i + 1).start()

    def gather_last(c):
        def body(j):
            fwd_copy(3, c, j).wait_recv()
            gather_in(3, c, j, fwd[fwd_at(3, c, j)])

        each(3, body)
        fwd_copy(3, c, 3).wait_recv()
        gather_in(3, c, 3, fwd[fwd_at(3, c, 3)], last=lambda i: y_start(c, i))

    send_own(0)
    loads[0].wait()
    densify(0)
    densify(1)
    relay_up(1, 0)
    pass_on(1, 0)
    send_own(1)
    densify(2)
    densify(3)
    relay_up(2, 0)
    pass_on(2, 0)
    relay_up(3, 0)
    loads[1].wait()
    gather_own()
    gather_slot(1, 0)
    relay_up(1, 1)
    gather_slot(2, 0)
    gather_last(0)
    relay_up(2, 1)
    pass_on(1, 1)
    gather_slot(1, 1)
    relay_up(3, 1)
    pass_on(2, 1)
    gather_slot(2, 1)

    loads[2].wait()
    for k in range(2):
        value = w_raw[pl.ds(k * HALF, HALF), :]
        w_hi[k], w_lo[k] = split(value)
        wt_hi[k], wt_lo[k] = split(value.T)
    loads[3].wait()
    gather_last(1)

    def near_part(i):
        rows = pl.ds(pl.multiple_of(i * 256, 256), 256)
        value = jnp.concatenate([agg[0, rows, :], agg[1, rows, :]], axis=1)
        pre[rows, :] = dot3(split(value), (w_hi[feat], w_lo[feat]))

    each(4, near_part)
    for i in range(4):
        y_copy(0, i).wait_recv()

    def far_part(c, i):
        rows = pl.ds(pl.multiple_of(i * 256, 256), 256)
        ks = pl.ds(c * LANES, LANES)
        return dot3(split(agg_far[c, rows, :]), (w_hi[other, ks, :], w_lo[other, ks, :]))

    def far_first(i):
        rows = pl.ds(pl.multiple_of(i * 256, 256), 256)
        pre[rows, :] += far_part(0, i)

    each(4, far_first)

    def activate(i):
        rows = pl.ds(pl.multiple_of(i * 256, 256), 256)
        y_copy(1, i).wait_recv()
        value = pre[rows, :] + far_part(1, i)
        s = jax.nn.sigmoid(value)
        act[rows, :] = value * s
        grad = cot[rows, :] * (s + value * s * (1.0 - s))
        pgt[:HALF, rows], pgt[HALF:, rows] = split(grad.T)

    each(4, activate)
    act_copy = pltpu.make_async_copy(act, act_out, local_sem.at[4])
    act_copy.start()

    def times_pgt(high, low):
        both = dot(pgt[...], high)
        return both[:HALF] + both[HALF:] + dot(pgt[:HALF, :], low)

    def term(w, j, count):
        n = w * GRID + j
        if count == 1:
            return times_pgt(adj_hi[n], adj_lo[n])
        return times_pgt(
            jnp.concatenate([adj_hi[n], adj_hi[n + 1]], axis=1),
            jnp.concatenate([adj_lo[n], adj_lo[n + 1]], axis=1),
        )

    def z_copy(s, j):
        n = s * GRID + j
        return remote(z_send.at[n], z_recv.at[n], z_ss.at[n], z_rs.at[n], down)

    def z_detour(s, j):
        n = s * GRID + j
        k = s * (GRID // 2) + j // 2
        return remote(z_send.at[n], z_relay.at[k], z_ss.at[n], z_in.at[k], down_relay)

    def z_resend(s, j):
        n = s * GRID + j
        k = s * (GRID // 2) + j // 2
        return remote(z_relay.at[k], z_recv.at[n], z_on.at[k], z_rs.at[n], down_relay_on)

    def z_start(s, j, odd):
        if odd:
            pl.when(wraps_down)(lambda: z_detour(s, j).start())
            pl.when(jnp.logical_not(wraps_down))(lambda: z_copy(s, j).start())
        else:
            z_copy(s, j).start()

    def carried(s, j, odd):
        if odd:
            def run():
                z_detour(s, j).wait_recv()
                z_resend(s, j).start()

            pl.when(relays_down)(run)
        z_copy(s, j).wait_recv()
        return z_recv[s * GRID + j]

    def z_step(s, pair):
        value = term(3 - s, 2 * pair, 2)
        for h in range(2):
            j = 2 * pair + h
            part = value[:, h * LANES:(h + 1) * LANES]
            if s > 0:
                part = part + carried(s - 1, j, h == 1)
            z_send[s * GRID + j] = part
            z_start(s, j, h == 1)

    def f_copy(j):
        return remote(f_send.at[j], f_recv.at[j], f_ss.at[j], f_rs.at[j], mate)

    def last_step(start, odds):
        count = len(odds)
        value = term(0, start, count)
        sums = [
            value[:, h * LANES:(h + 1) * LANES] + carried(2, start + h, odd)
            for h, odd in enumerate(odds)
        ]
        parts = split(jnp.concatenate(sums, axis=1).T)
        far = dot3(parts, (wt_hi[other], wt_lo[other]))
        for h in range(count):
            f_send[start + h] = far[h * LANES:(h + 1) * LANES]
            f_copy(start + h).start()
        near = dot3(parts, (wt_hi[feat], wt_lo[feat]))
        for h in range(count):
            f_own[start + h] = near[h * LANES:(h + 1) * LANES]

    scale = F32(1.0 / math.sqrt(ROWS * PARTS))

    def weight_part(source, half):
        high, low = split(jnp.concatenate([source[0], source[1]], axis=1))
        grad = times_pgt(high, low).T * scale
        for h in range(2):
            start = pl.multiple_of(h * 512 + half * HALF, HALF)
            ar[pl.ds(start, HALF), :] = grad[:, h * LANES:(h + 1) * LANES]

    def rows_at(start, size, ref):
        return ref.at[pl.ds(pl.multiple_of(start, 8), size)]

    def read_at(start, size, ref):
        return ref[pl.ds(pl.multiple_of(start, 8), size), :]

    def sum_core():
        return remote(rows_at((1 - core) * 512, 512, ar), ar_core, ar_ss.at[0], ar_rs.at[0], core_peer)

    def sum_x(d):
        return remote(
            rows_at(x_peer(d) * 128, 128, s1), ar_x.at[d - 1], ar_ss.at[d], ar_rs.at[d],
            at(x_peer(d), y, z, core),
        )

    def sum_y():
        return remote(rows_at((1 - y) * 64, 64, s2), ar_y, ar_ss.at[4], ar_rs.at[4], y_peer)

    def sum_z(d):
        return remote(
            rows_at(z_peer(d) * 8, 8, s3), ar_z.at[d - 1], ar_ss.at[4 + d], ar_rs.at[4 + d],
            at(x, y, z_peer(d), core),
        )

    base_core = core * 512
    base_x = base_core + x * 128
    base_y = base_x + y * 64
    base_z = base_y + z * 8

    def share(base, size, n, device):
        return remote(rows_at(base, size, ag), rows_at(base, size, ag), ag_ss.at[n], ag_rs.at[n], device)

    def share_z(d):
        return share(base_z, 8, d - 1, at(x, y, z_peer(d), core))

    def share_y():
        return share(base_y, 64, 7, y_peer)

    def share_x(d):
        return share(base_x, 128, 7 + d, at(x_peer(d), y, z, core))

    def share_core():
        return share(base_core, 512, 11, core_peer)

    def landed_z(d):
        peer = lax.rem(z + Z - d, Z)
        return share(base_y + peer * 8, 8, d - 1, mate)

    def landed_y():
        return share(base_x + (1 - y) * 64, 64, 7, mate)

    def landed_x(d):
        peer = lax.rem(x + X - d, X)
        return share(base_core + peer * 128, 128, 7 + d, mate)

    def landed_core():
        return share((1 - core) * 512, 512, 11, mate)

    def point0():
        sum_core().start()

    def point1():
        sum_core().wait_recv()
        s1[...] = read_at(base_core, 512, ar) + ar_core[...]
        for d in range(1, X):
            sum_x(d).start()

    def point2():
        total = read_at(x * 128, 128, s1)
        for d in range(1, X):
            sum_x(d).wait_recv()
            total = total + ar_x[d - 1]
        s2[...] = total
        sum_y().start()

    def point3():
        sum_y().wait_recv()
        s3[...] = read_at(y * 64, 64, s2) + ar_y[...]
        for d in range(1, Z):
            sum_z(d).start()

    def point4():
        total = read_at(z * 8, 8, s3)
        for d in range(1, Z):
            sum_z(d).wait_recv()
            total = total + ar_z[d - 1]
        ag[pl.ds(pl.multiple_of(base_z, 8), 8), :] = total
        for d in range(1, Z):
            share_z(d).start()

    def point5():
        for d in range(1, Z):
            landed_z(d).wait_recv()
        share_y().start()

    def point6():
        landed_y().wait_recv()
        for d in range(1, X):
            share_x(d).start()

    def point7():
        for d in range(1, X):
            landed_x(d).wait_recv()
        share_core().start()

    wgrad_copies = [
        pltpu.make_async_copy(
            ag.at[pl.ds(h * 512, 512)], wgrad_out.at[:, pl.ds(h * LANES, LANES)], local_sem.at[(5, 14)[h]]
        )
        for h in range(2)
    ]

    def point8():
        landed_core().wait_recv()
        for copy in wgrad_copies:
            copy.start()

    late = first_z | (z >= Z - 2)
    soon = jnp.logical_not(late)

    def after(i, points, where):
        for k, point in points.items():
            pl.when((i == k) & where)(point)

    def third(i):
        z_step(2, i)
        after(i, {1: point3}, is_even)
        after(i, {0: point3}, is_odd)
        after(i, {2: point4, 3: point5}, is_odd & late)
        after(i, {3: point4}, is_even & late)

    def fourth(i):
        last_step(2 * i, (False, True))
        after(i, {0: point6, 1: point7}, is_odd & late)
        after(i, {0: point5, 1: point6, 2: point7}, is_even & late)
        after(i, {0: point4, 1: point5, 2: point6}, is_odd & soon)

    def even_end():
        point4()
        point5()
        point6()

    def second(i):
        z_step(1, i)
        after(i, {1: point1, 3: point2}, is_odd)

    def both12():
        point1()
        point2()

    each(4, lambda i: z_step(0, i))
    weight_part(agg, feat)
    weight_part(agg_far, other)
    point0()
    each(4, second)
    pl.when(is_even)(both12)
    each(4, third)
    each(3, fourth)
    last_step(6, (False,))
    last_step(7, (True,))
    pl.when(is_even & soon)(even_end)
    pl.when(soon)(point7)

    def finish(j):
        f_copy(j).wait_recv()
        f_own[j] += f_recv[j]
        rows = pl.ds(pl.multiple_of(j * LANES, LANES), LANES)
        pltpu.make_async_copy(f_own.at[j], grad_out.at[rows], local_sem.at[6 + j]).start()

    each(GRID, finish)
    point8()

    for c in range(2):
        for w in range(1, SLOTS):
            for j in range(4):
                fwd_copy(w, c, j).wait_send()
            pl.when(relays_up)(lambda w=w, c=c: [fwd_resend(w, c, j).wait_send() for j in (1, 3)] and None)
        for i in range(4):
            y_copy(c, i).wait_send()

    def sent(j):
        for s in range(3):
            z_copy(s, j).wait_send()
            pl.when(relays_down & (lax.rem(j, 2) == 1))(lambda s=s: z_resend(s, j).wait_send())
        f_copy(j).wait_send()

    each(GRID, sent)
    sum_core().wait_send()
    sum_y().wait_send()
    share_core().wait_send()
    share_y().wait_send()
    for d in range(1, X):
        sum_x(d).wait_send()
        share_x(d).wait_send()
    for d in range(1, Z):
        sum_z(d).wait_send()
        share_z(d).wait_send()
    act_copy.wait()
    for copy in wgrad_copies:
        copy.wait()

    def written(j):
        rows = pl.ds(pl.multiple_of(j * LANES, LANES), LANES)
        pltpu.make_async_copy(f_own.at[j], grad_out.at[rows], local_sem.at[6 + j]).wait()

    each(GRID, written)


def copy_kernel(a_in, b_in, c_in, a_out, b_out, c_out, a, b, c, sems):
    groups = ((a_in, a, a_out), (b_in, b, b_out), (c_in, c, c_out))
    reads, writes = [], []
    for i, (src, mid, dst) in enumerate(groups):
        size = src.shape[0] // 4
        for k in range(4):
            rows = pl.ds(k * size, size)
            reads.append(pltpu.make_async_copy(src.at[rows], mid.at[rows], sems.at[i * 4 + k]))
            writes.append(pltpu.make_async_copy(mid.at[rows], dst.at[rows], sems.at[12 + i * 4 + k]))
    for read in reads:
        read.start()
    for read, write in zip(reads, writes):
        read.wait()
        write.start()
    for write in writes:
        write.wait()


def body(features, weight, cotangent, block_rows, block_cols, block_counts, block_values):
    order = jnp.arange(CAP, dtype=jnp.int32)
    live = order[None, :] < block_counts[0][:, None]
    place = jnp.where(live, block_rows[0] * GRID + block_cols[0], -1)
    hit = place[:, None, :] == jnp.arange(GRID * GRID, dtype=jnp.int32)[None, :, None]
    table = jnp.max(jnp.where(hit, order[None, None, :], -1), axis=2).reshape(-1)
    vmem = pltpu.VMEM
    dma = pltpu.SemaphoreType.DMA
    anywhere = pl.BlockSpec(memory_space=pl.ANY)
    results = pl.pallas_call(
        kernel,
        out_shape=(
            jax.ShapeDtypeStruct((ROWS, HALF), F32),
            jax.ShapeDtypeStruct((ROWS, HALF), F32),
            jax.ShapeDtypeStruct((2 * HALF, HALF), F32),
        ),
        in_specs=[pl.BlockSpec(memory_space=pltpu.SMEM)] + [anywhere] * 4,
        out_specs=(anywhere,) * 3,
        scratch_shapes=[
            vmem((SLOTS * CAP, LANES, LANES), F32),
            vmem((SLOTS * GRID, ROWS, LANES), BF16),
            vmem((SLOTS * GRID, ROWS, LANES), BF16),
            vmem((ROWS, HALF), F32),
            vmem((2 * HALF, HALF), F32),
            vmem((2, HALF, HALF), BF16),
            vmem((2, HALF, HALF), BF16),
            vmem((2, HALF, HALF), BF16),
            vmem((2, HALF, HALF), BF16),
            vmem((ROWS, HALF), F32),
            vmem((24, 256, LANES), F32),
            vmem((ROWS, HALF), BF16),
            vmem((ROWS, HALF), BF16),
            vmem((2, ROWS, LANES), F32),
            vmem((2, ROWS, LANES), F32),
            vmem((ROWS, HALF), F32),
            vmem((ROWS, HALF), F32),
            vmem((2 * HALF, ROWS), BF16),
            vmem((3 * GRID, HALF, LANES), F32),
            vmem((3 * GRID, HALF, LANES), F32),
            vmem((GRID, LANES, HALF), F32),
            vmem((GRID, LANES, HALF), F32),
            vmem((GRID, LANES, HALF), F32),
            vmem((1024, LANES), F32),
            vmem((512, LANES), F32),
            vmem((512, LANES), F32),
            vmem((3, 128, LANES), F32),
            vmem((128, LANES), F32),
            vmem((64, LANES), F32),
            vmem((64, LANES), F32),
            vmem((7, 8, LANES), F32),
            vmem((1024, LANES), F32),
            vmem((12, 256, LANES), F32),
            vmem((12, HALF, LANES), F32),
            dma((15,)),
            dma((24,)), dma((24,)),
            dma((8,)), dma((8,)),
            dma((24,)), dma((24,)),
            dma((8,)), dma((8,)),
            dma((12,)), dma((12,)), dma((12,)), dma((12,)),
            dma((12,)), dma((12,)),
            dma((12,)), dma((12,)),
        ],
        compiler_params=pltpu.CompilerParams(
            collective_id=0, has_side_effects=True, vmem_limit_bytes=56 * 2**20
        ),
        cost_estimate=pl.CostEstimate(flops=16 * 10**9, bytes_accessed=12 * 2**20, transcendentals=ROWS * HALF),
        name="layer",
    )(table, features, weight, cotangent, block_values.reshape(SLOTS * CAP, LANES, LANES))
    return pl.pallas_call(
        copy_kernel,
        out_shape=tuple(jax.ShapeDtypeStruct(r.shape, F32) for r in results),
        in_specs=[anywhere] * 3,
        out_specs=(anywhere,) * 3,
        scratch_shapes=[vmem(r.shape, F32) for r in results] + [dma((24,))],
        name="results",
    )(*results)


def solution(mesh):
    in_specs = (
        P("dom", "feat"),
        P(None, "feat"),
        P("dom", "feat"),
        P("dom", None, None),
        P("dom", None, None),
        P("dom", None),
        P("dom", None, None, None, None),
    )
    out_specs = (P("dom", "feat"), P("dom", "feat"), P(None, "feat"))
    return jax.shard_map(body, mesh=mesh, in_specs=in_specs, out_specs=out_specs, check_vma=False)
```

```python
import math

import jax
import jax.numpy as jnp
from jax import lax
from jax.experimental import pallas as pl
from jax.experimental.pallas import tpu as pltpu
from jax.sharding import PartitionSpec as P

MESH = pl.DeviceIdType.MESH
F32 = jnp.float32
BF16 = jnp.bfloat16
X, Y, Z, CORES = 4, 2, 8, 2
PARTS = X * Y * Z * CORES
SLOTS, CAP, GRID = 4, 24, 8
ROWS, HALF, LANES = 1024, 256, 128


def split(value):
    high = value.astype(BF16)
    return high, (value - high.astype(F32)).astype(BF16)


def dot(a, b):
    return jnp.dot(a, b, preferred_element_type=F32)


def dot3(a, b):
    return dot(a[0], b[0]) + dot(a[1], b[0]) + dot(a[0], b[1])


def remote(src, dst, send, recv, device):
    return pltpu.make_async_remote_copy(
        src_ref=src, dst_ref=dst, send_sem=send, recv_sem=recv,
        device_id=device, device_id_type=MESH,
    )


def kernel(
    block_rows, block_cols, block_counts, features, weight, cotangent, blocks_in,
    act_out, grad_out, wgrad_out,
    blocks, adj_hi, adj_lo, own, w_raw, w_hi, w_lo, wt_hi, wt_lo, cot,
    fwd, side_hi, side_lo, agg, agg_far, pre, act, pgt,
    z_send, z_recv, f_send, f_recv, f_own,
    ar, ar_core, s1, ar_x, s2, ar_y, s3, ar_z, ag,
    fwd_relay, z_relay, place,
    local_sem, fwd_ss, fwd_rs, y_ss, y_rs, z_ss, z_rs, f_ss, f_rs,
    fwd_in, fwd_on, z_in, z_on,
    ar_ss, ar_rs, ag_ss, ag_rs,
):
    me = lax.axis_index("dom")
    feat = lax.axis_index("feat")
    other = 1 - feat
    core = lax.rem(me, 2)
    z = lax.rem(me // 2, Z)
    y = lax.rem(me // (2 * Z), Y)
    x = me // (2 * Z * Y)
    up = (lax.rem(me + 1, PARTS), feat)
    down = (lax.rem(me + PARTS - 1, PARTS), feat)
    mate = (me, other)

    def at(x_, y_, z_, core_):
        return (((x_ * Y + y_) * Z + z_) * 2 + core_, feat)

    core_peer = at(x, y, z, 1 - core)
    x_next, x_before = lax.rem(x + y, X), lax.rem(x + y + X - 1, X)
    first_z, last_z = z == 0, z == Z - 1
    is_odd, is_even = core == 1, core == 0
    wraps_up, wraps_down = is_odd & last_z, is_even & first_z
    relays_up, relays_down = is_even & last_z, is_odd & first_z
    up_relay = at(x_next, 1 - y, Z - 1, 0)
    up_relay_on = at(x, y, 0, 0)
    down_relay = at(x_before, 1 - y, 0, 1)
    down_relay_on = at(x, y, Z - 1, 1)
    y_peer = at(x, 1 - y, z, core)

    def x_peer(d):
        return lax.rem(x + d, X)

    def z_peer(d):
        return lax.rem(z + d, Z)

    loads = [
        pltpu.make_async_copy(blocks_in, blocks, local_sem.at[0]),
        pltpu.make_async_copy(features, own, local_sem.at[1]),
        pltpu.make_async_copy(weight, w_raw, local_sem.at[2]),
        pltpu.make_async_copy(cotangent, cot, local_sem.at[3]),
    ]
    for load in loads:
        load.start()

    barrier = pltpu.get_barrier_semaphore()
    partners = [up, down, mate, y_peer]
    partners += [at(x_peer(d), y, z, core) for d in range(1, X)]
    partners += [at(x, y, z_peer(d), core) for d in range(1, Z)]
    partners += [at(x_next, 1 - y, z, 1 - core), at(x_before, 1 - y, z, 1 - core)]
    for partner in partners:
        pl.semaphore_signal(barrier, inc=1, device_id=partner, device_id_type=MESH)
    pl.semaphore_wait(barrier, len(partners))

    def fwd_at(w, c, j):
        return ((w - 1) * 2 + c) * 4 + j

    def fwd_copy(w, c, j):
        i = fwd_at(w, c, j)
        if w == 1:
            src = features.at[pl.ds(j * 256, 256), pl.ds(c * LANES, LANES)]
        else:
            src = fwd.at[fwd_at(w - 1, c, j)]
        return remote(src, fwd.at[i], fwd_ss.at[i], fwd_rs.at[i], up)

    def fwd_detour(w, c, j):
        i = fwd_at(w, c, j)
        if w == 1:
            src = features.at[pl.ds(j * 256, 256), pl.ds(c * LANES, LANES)]
        else:
            src = fwd.at[fwd_at(w - 1, c, j)]
        n = fwd_at(w, c, 0) // 2 + j // 2
        return remote(src, fwd_relay.at[n], fwd_ss.at[i], fwd_in.at[n], up_relay)

    def fwd_resend(w, c, j):
        i = fwd_at(w, c, j)
        n = fwd_at(w, c, 0) // 2 + j // 2
        return remote(fwd_relay.at[n], fwd.at[i], fwd_on.at[n], fwd_rs.at[i], up_relay_on)

    def fwd_start(w, c, j):
        if j % 2 == 0:
            fwd_copy(w, c, j).start()
        else:
            pl.when(wraps_up)(lambda: fwd_detour(w, c, j).start())
            pl.when(jnp.logical_not(wraps_up))(lambda: fwd_copy(w, c, j).start())

    def relay_up(w, c):
        def run():
            for j in (1, 3):
                fwd_detour(w, c, j).wait_recv()
                fwd_resend(w, c, j).start()

        pl.when(relays_up)(run)

    def each(n, body, start=0):
        def step(j, carry):
            body(j)
            return carry

        lax.fori_loop(start, start + n, step, 0)

    def send_own(c):
        for j in range(4):
            fwd_start(1, c, j)

    def pass_on(w, c):
        for j in range(4):
            fwd_copy(w, c, j).wait_recv()
            fwd_start(w + 1, c, j)

    def densify(w):
        for k in range(CAP):
            at_k = block_rows[0, w, k] * GRID + block_cols[0, w, k]
            place[k] = jnp.where(k < block_counts[0, w], at_k, -1)

        def body(r):
            rows = pl.ds(pl.multiple_of(r * LANES, LANES), LANES)
            for c in range(GRID):
                found = jnp.int32(-1)
                for k in range(CAP):
                    found = jnp.where(place[k] == r * GRID + c, k, found)
                live = jnp.where(found >= 0, 1.0, 0.0).astype(F32)
                high, low = split(blocks[w * CAP + jnp.maximum(found, 0)] * live)
                adj_hi[w * GRID + c, rows, :] = high
                adj_lo[w * GRID + c, rows, :] = low

        each(GRID, body)

    def gather_in(w, c, j, piece, last=None):
        high, low = split(piece)
        both = jnp.concatenate([high, low], axis=1)

        def body(i):
            rows = pl.ds(pl.multiple_of(i * 512, 512), 512)
            a_hi = jnp.concatenate(
                [adj_hi[w * GRID + 2 * j, rows, :], adj_hi[w * GRID + 2 * j + 1, rows, :]], axis=1
            )
            a_lo = jnp.concatenate(
                [adj_lo[w * GRID + 2 * j, rows, :], adj_lo[w * GRID + 2 * j + 1, rows, :]], axis=1
            )
            wide = dot(a_hi, both)
            total = wide[:, :LANES] + wide[:, LANES:] + dot(a_lo, high)
            agg[c, rows, :] += total
            if last is not None:
                last(i)

        each(2, body)

    def tile(adj, w, i):
        rows = pl.ds(pl.multiple_of(i * 256, 256), 256)
        return jnp.concatenate([adj[w * GRID + k, rows, :] for k in range(GRID)], axis=1)

    def gather_own():
        for c in range(2):
            high, low = split(own[:, c * LANES:(c + 1) * LANES])
            side_hi[:, c * LANES:(c + 1) * LANES] = high
            side_lo[:, c * LANES:(c + 1) * LANES] = low

        def body(i):
            a_hi, a_lo = tile(adj_hi, 0, i), tile(adj_lo, 0, i)
            total = dot(a_hi, side_hi[...]) + dot(a_hi, side_lo[...]) + dot(a_lo, side_hi[...])
            rows = pl.ds(pl.multiple_of(i * 256, 256), 256)
            for c in range(2):
                agg[c, rows, :] = total[:, c * LANES:(c + 1) * LANES]

        each(4, body)

    def gather_slot(w, c):
        for j in range(4):
            high, low = split(fwd[fwd_at(w, c, j)])
            side_hi[j * 256:(j + 1) * 256, :LANES] = high
            side_hi[j * 256:(j + 1) * 256, LANES:] = low

        def body(i):
            wide = dot(tile(adj_hi, w, i), side_hi[...])
            rest = dot(tile(adj_lo, w, i), side_hi[:, :LANES])
            rows = pl.ds(pl.multiple_of(i * 256, 256), 256)
            agg[c, rows, :] += wide[:, :LANES] + wide[:, LANES:] + rest

        each(4, body)

    def y_copy(c, i):
        rows = pl.ds(pl.multiple_of(i * 256, 256), 256)
        n = c * 4 + i
        return remote(agg.at[c, rows], agg_far.at[c, rows], y_ss.at[n], y_rs.at[n], mate)

    def y_start(c, i):
        y_copy(c, 2 * i).start()
        y_copy(c, 2 * i + 1).start()

    def gather_last(c):
        def body(j):
            fwd_copy(3, c, j).wait_recv()
            gather_in(3, c, j, fwd[fwd_at(3, c, j)])

        each(3, body)
        fwd_copy(3, c, 3).wait_recv()
        gather_in(3, c, 3, fwd[fwd_at(3, c, 3)], last=lambda i: y_start(c, i))

    send_own(0)
    loads[0].wait()
    densify(0)
    relay_up(1, 0)
    pass_on(1, 0)
    send_own(1)
    densify(1)
    densify(2)
    densify(3)
    relay_up(2, 0)
    pass_on(2, 0)
    relay_up(3, 0)
    loads[1].wait()
    gather_own()
    gather_slot(1, 0)
    relay_up(1, 1)
    gather_slot(2, 0)
    gather_last(0)
    relay_up(2, 1)
    pass_on(1, 1)
    gather_slot(1, 1)
    relay_up(3, 1)
    pass_on(2, 1)
    gather_slot(2, 1)

    loads[2].wait()
    for k in range(2):
        value = w_raw[pl.ds(k * HALF, HALF), :]
        w_hi[k], w_lo[k] = split(value)
        wt_hi[k], wt_lo[k] = split(value.T)
    loads[3].wait()
    gather_last(1)

    def near_part(i):
        rows = pl.ds(pl.multiple_of(i * 256, 256), 256)
        value = jnp.concatenate([agg[0, rows, :], agg[1, rows, :]], axis=1)
        pre[rows, :] = dot3(split(value), (w_hi[feat], w_lo[feat]))

    each(4, near_part)
    for i in range(4):
        y_copy(0, i).wait_recv()

    def far_part(c, i):
        rows = pl.ds(pl.multiple_of(i * 256, 256), 256)
        ks = pl.ds(c * LANES, LANES)
        return dot3(split(agg_far[c, rows, :]), (w_hi[other, ks, :], w_lo[other, ks, :]))

    def far_first(i):
        rows = pl.ds(pl.multiple_of(i * 256, 256), 256)
        pre[rows, :] += far_part(0, i)

    each(4, far_first)

    def activate(i):
        rows = pl.ds(pl.multiple_of(i * 256, 256), 256)
        y_copy(1, i).wait_recv()
        value = pre[rows, :] + far_part(1, i)
        s = jax.nn.sigmoid(value)
        act[rows, :] = value * s
        grad = cot[rows, :] * (s + value * s * (1.0 - s))
        pgt[:HALF, rows], pgt[HALF:, rows] = split(grad.T)

    each(4, activate)
    act_copy = pltpu.make_async_copy(act, act_out, local_sem.at[4])
    act_copy.start()

    def times_pgt(high, low):
        both = dot(pgt[...], high)
        return both[:HALF] + both[HALF:] + dot(pgt[:HALF, :], low)

    def term(w, j, count):
        n = w * GRID + j
        if count == 1:
            return times_pgt(adj_hi[n], adj_lo[n])
        return times_pgt(
            jnp.concatenate([adj_hi[n], adj_hi[n + 1]], axis=1),
            jnp.concatenate([adj_lo[n], adj_lo[n + 1]], axis=1),
        )

    def z_copy(s, j):
        n = s * GRID + j
        return remote(z_send.at[n], z_recv.at[n], z_ss.at[n], z_rs.at[n], down)

    def z_detour(s, j):
        n = s * GRID + j
        k = s * (GRID // 2) + j // 2
        return remote(z_send.at[n], z_relay.at[k], z_ss.at[n], z_in.at[k], down_relay)

    def z_resend(s, j):
        n = s * GRID + j
        k = s * (GRID // 2) + j // 2
        return remote(z_relay.at[k], z_recv.at[n], z_on.at[k], z_rs.at[n], down_relay_on)

    def z_start(s, j, odd):
        if odd:
            pl.when(wraps_down)(lambda: z_detour(s, j).start())
            pl.when(jnp.logical_not(wraps_down))(lambda: z_copy(s, j).start())
        else:
            z_copy(s, j).start()

    def carried(s, j, odd):
        if odd:
            def run():
                z_detour(s, j).wait_recv()
                z_resend(s, j).start()

            pl.when(relays_down)(run)
        z_copy(s, j).wait_recv()
        return z_recv[s * GRID + j]

    def z_step(s, pair):
        value = term(3 - s, 2 * pair, 2)
        for h in range(2):
            j = 2 * pair + h
            part = value[:, h * LANES:(h + 1) * LANES]
            if s > 0:
                part = part + carried(s - 1, j, h == 1)
            z_send[s * GRID + j] = part
            z_start(s, j, h == 1)

    def f_copy(j):
        return remote(f_send.at[j], f_recv.at[j], f_ss.at[j], f_rs.at[j], mate)

    def last_step(start, odds):
        count = len(odds)
        value = term(0, start, count)
        sums = [
            value[:, h * LANES:(h + 1) * LANES] + carried(2, start + h, odd)
            for h, odd in enumerate(odds)
        ]
        parts = split(jnp.concatenate(sums, axis=1).T)
        far = dot3(parts, (wt_hi[other], wt_lo[other]))
        for h in range(count):
            f_send[start + h] = far[h * LANES:(h + 1) * LANES]
            f_copy(start + h).start()
        near = dot3(parts, (wt_hi[feat], wt_lo[feat]))
        for h in range(count):
            f_own[start + h] = near[h * LANES:(h + 1) * LANES]

    scale = F32(1.0 / math.sqrt(ROWS * PARTS))

    def weight_part(source, half):
        high, low = split(jnp.concatenate([source[0], source[1]], axis=1))
        grad = times_pgt(high, low).T * scale
        for h in range(2):
            start = pl.multiple_of(h * 512 + half * HALF, HALF)
            ar[pl.ds(start, HALF), :] = grad[:, h * LANES:(h + 1) * LANES]

    def rows_at(start, size, ref):
        return ref.at[pl.ds(pl.multiple_of(start, 8), size)]

    def read_at(start, size, ref):
        return ref[pl.ds(pl.multiple_of(start, 8), size), :]

    def sum_core():
        return remote(rows_at((1 - core) * 512, 512, ar), ar_core, ar_ss.at[0], ar_rs.at[0], core_peer)

    def sum_x(d):
        return remote(
            rows_at(x_peer(d) * 128, 128, s1), ar_x.at[d - 1], ar_ss.at[d], ar_rs.at[d],
            at(x_peer(d), y, z, core),
        )

    def sum_y():
        return remote(rows_at((1 - y) * 64, 64, s2), ar_y, ar_ss.at[4], ar_rs.at[4], y_peer)

    def sum_z(d):
        return remote(
            rows_at(z_peer(d) * 8, 8, s3), ar_z.at[d - 1], ar_ss.at[4 + d], ar_rs.at[4 + d],
            at(x, y, z_peer(d), core),
        )

    base_core = core * 512
    base_x = base_core + x * 128
    base_y = base_x + y * 64
    base_z = base_y + z * 8

    def share(base, size, n, device):
        return remote(rows_at(base, size, ag), rows_at(base, size, ag), ag_ss.at[n], ag_rs.at[n], device)

    def share_z(d):
        return share(base_z, 8, d - 1, at(x, y, z_peer(d), core))

    def share_y():
        return share(base_y, 64, 7, y_peer)

    def share_x(d):
        return share(base_x, 128, 7 + d, at(x_peer(d), y, z, core))

    def share_core():
        return share(base_core, 512, 11, core_peer)

    def landed_z(d):
        peer = lax.rem(z + Z - d, Z)
        return share(base_y + peer * 8, 8, d - 1, mate)

    def landed_y():
        return share(base_x + (1 - y) * 64, 64, 7, mate)

    def landed_x(d):
        peer = lax.rem(x + X - d, X)
        return share(base_core + peer * 128, 128, 7 + d, mate)

    def landed_core():
        return share((1 - core) * 512, 512, 11, mate)

    def point0():
        sum_core().start()

    def point1():
        sum_core().wait_recv()
        s1[...] = read_at(base_core, 512, ar) + ar_core[...]
        for d in range(1, X):
            sum_x(d).start()

    def point2():
        total = read_at(x * 128, 128, s1)
        for d in range(1, X):
            sum_x(d).wait_recv()
            total = total + ar_x[d - 1]
        s2[...] = total
        sum_y().start()

    def point3():
        sum_y().wait_recv()
        s3[...] = read_at(y * 64, 64, s2) + ar_y[...]
        for d in range(1, Z):
            sum_z(d).start()

    def point4():
        total = read_at(z * 8, 8, s3)
        for d in range(1, Z):
            sum_z(d).wait_recv()
            total = total + ar_z[d - 1]
        ag[pl.ds(pl.multiple_of(base_z, 8), 8), :] = total
        for d in range(1, Z):
            share_z(d).start()

    def point5():
        for d in range(1, Z):
            landed_z(d).wait_recv()
        share_y().start()

    def point6():
        landed_y().wait_recv()
        for d in range(1, X):
            share_x(d).start()

    def point7():
        for d in range(1, X):
            landed_x(d).wait_recv()
        share_core().start()

    wgrad_copies = [
        pltpu.make_async_copy(
            ag.at[pl.ds(h * 512, 512)], wgrad_out.at[:, pl.ds(h * LANES, LANES)], local_sem.at[(5, 14)[h]]
        )
        for h in range(2)
    ]

    def point8():
        landed_core().wait_recv()
        for copy in wgrad_copies:
            copy.start()

    late = first_z | (z >= Z - 2)
    soon = jnp.logical_not(late)

    def after(i, points, where):
        for k, point in points.items():
            pl.when((i == k) & where)(point)

    def third(i):
        z_step(2, i)
        after(i, {1: point3}, is_even)
        after(i, {0: point3}, is_odd)
        after(i, {2: point4, 3: point5}, is_odd & late)
        after(i, {3: point4}, is_even & late)

    def fourth(i):
        last_step(2 * i, (False, True))
        after(i, {0: point6, 1: point7}, is_odd & late)
        after(i, {0: point5, 1: point6, 2: point7}, is_even & late)
        after(i, {0: point4, 1: point5, 2: point6}, is_odd & soon)

    def even_end():
        point4()
        point5()
        point6()

    def second(i):
        z_step(1, i)
        after(i, {1: point1, 3: point2}, is_odd)

    def both12():
        point1()
        point2()

    each(4, lambda i: z_step(0, i))
    weight_part(agg, feat)
    weight_part(agg_far, other)
    point0()
    each(4, second)
    pl.when(is_even)(both12)
    each(4, third)
    each(3, fourth)
    last_step(6, (False,))
    last_step(7, (True,))
    pl.when(is_even & soon)(even_end)
    pl.when(soon)(point7)

    def finish(j):
        f_copy(j).wait_recv()
        f_own[j] += f_recv[j]
        rows = pl.ds(pl.multiple_of(j * LANES, LANES), LANES)
        pltpu.make_async_copy(f_own.at[j], grad_out.at[rows], local_sem.at[6 + j]).start()

    each(GRID, finish)
    point8()

    for c in range(2):
        for w in range(1, SLOTS):
            for j in range(4):
                fwd_copy(w, c, j).wait_send()
            pl.when(relays_up)(lambda w=w, c=c: [fwd_resend(w, c, j).wait_send() for j in (1, 3)] and None)
        for i in range(4):
            y_copy(c, i).wait_send()

    def sent(j):
        for s in range(3):
            z_copy(s, j).wait_send()
            pl.when(relays_down & (lax.rem(j, 2) == 1))(lambda s=s: z_resend(s, j).wait_send())
        f_copy(j).wait_send()

    each(GRID, sent)
    sum_core().wait_send()
    sum_y().wait_send()
    share_core().wait_send()
    share_y().wait_send()
    for d in range(1, X):
        sum_x(d).wait_send()
        share_x(d).wait_send()
    for d in range(1, Z):
        sum_z(d).wait_send()
        share_z(d).wait_send()
    act_copy.wait()
    for copy in wgrad_copies:
        copy.wait()

    def written(j):
        rows = pl.ds(pl.multiple_of(j * LANES, LANES), LANES)
        pltpu.make_async_copy(f_own.at[j], grad_out.at[rows], local_sem.at[6 + j]).wait()

    each(GRID, written)


def copy_kernel(a_in, b_in, c_in, a_out, b_out, c_out, a, b, c, sems):
    groups = ((a_in, a, a_out), (b_in, b, b_out), (c_in, c, c_out))
    reads, writes = [], []
    for i, (src, mid, dst) in enumerate(groups):
        size = src.shape[0] // 4
        for k in range(4):
            rows = pl.ds(k * size, size)
            reads.append(pltpu.make_async_copy(src.at[rows], mid.at[rows], sems.at[i * 4 + k]))
            writes.append(pltpu.make_async_copy(mid.at[rows], dst.at[rows], sems.at[12 + i * 4 + k]))
    for read in reads:
        read.start()
    for read, write in zip(reads, writes):
        read.wait()
        write.start()
    for write in writes:
        write.wait()


def body(features, weight, cotangent, block_rows, block_cols, block_counts, block_values):
    vmem = pltpu.VMEM
    dma = pltpu.SemaphoreType.DMA
    anywhere = pl.BlockSpec(memory_space=pl.ANY)
    results = pl.pallas_call(
        kernel,
        out_shape=(
            jax.ShapeDtypeStruct((ROWS, HALF), F32),
            jax.ShapeDtypeStruct((ROWS, HALF), F32),
            jax.ShapeDtypeStruct((2 * HALF, HALF), F32),
        ),
        in_specs=[pl.BlockSpec(memory_space=pltpu.SMEM)] * 3 + [anywhere] * 4,
        out_specs=(anywhere,) * 3,
        scratch_shapes=[
            vmem((SLOTS * CAP, LANES, LANES), F32),
            vmem((SLOTS * GRID, ROWS, LANES), BF16),
            vmem((SLOTS * GRID, ROWS, LANES), BF16),
            vmem((ROWS, HALF), F32),
            vmem((2 * HALF, HALF), F32),
            vmem((2, HALF, HALF), BF16),
            vmem((2, HALF, HALF), BF16),
            vmem((2, HALF, HALF), BF16),
            vmem((2, HALF, HALF), BF16),
            vmem((ROWS, HALF), F32),
            vmem((24, 256, LANES), F32),
            vmem((ROWS, HALF), BF16),
            vmem((ROWS, HALF), BF16),
            vmem((2, ROWS, LANES), F32),
            vmem((2, ROWS, LANES), F32),
            vmem((ROWS, HALF), F32),
            vmem((ROWS, HALF), F32),
            vmem((2 * HALF, ROWS), BF16),
            vmem((3 * GRID, HALF, LANES), F32),
            vmem((3 * GRID, HALF, LANES), F32),
            vmem((GRID, LANES, HALF), F32),
            vmem((GRID, LANES, HALF), F32),
            vmem((GRID, LANES, HALF), F32),
            vmem((1024, LANES), F32),
            vmem((512, LANES), F32),
            vmem((512, LANES), F32),
            vmem((3, 128, LANES), F32),
            vmem((128, LANES), F32),
            vmem((64, LANES), F32),
            vmem((64, LANES), F32),
            vmem((7, 8, LANES), F32),
            vmem((1024, LANES), F32),
            vmem((12, 256, LANES), F32),
            vmem((12, HALF, LANES), F32),
            pltpu.SMEM((CAP,), jnp.int32),
            dma((15,)),
            dma((24,)), dma((24,)),
            dma((8,)), dma((8,)),
            dma((24,)), dma((24,)),
            dma((8,)), dma((8,)),
            dma((12,)), dma((12,)), dma((12,)), dma((12,)),
            dma((12,)), dma((12,)),
            dma((12,)), dma((12,)),
        ],
        compiler_params=pltpu.CompilerParams(
            collective_id=0, has_side_effects=True, vmem_limit_bytes=56 * 2**20
        ),
        cost_estimate=pl.CostEstimate(flops=16 * 10**9, bytes_accessed=12 * 2**20, transcendentals=ROWS * HALF),
        name="layer",
    )(block_rows, block_cols, block_counts, features, weight, cotangent, block_values.reshape(SLOTS * CAP, LANES, LANES))
    return pl.pallas_call(
        copy_kernel,
        out_shape=tuple(jax.ShapeDtypeStruct(r.shape, F32) for r in results),
        in_specs=[anywhere] * 3,
        out_specs=(anywhere,) * 3,
        scratch_shapes=[vmem(r.shape, F32) for r in results] + [dma((24,))],
        name="results",
    )(*results)


def solution(mesh):
    in_specs = (
        P("dom", "feat"),
        P(None, "feat"),
        P("dom", "feat"),
        P("dom", None, None),
        P("dom", None, None),
        P("dom", None),
        P("dom", None, None, None, None),
    )
    out_specs = (P("dom", "feat"), P("dom", "feat"), P(None, "feat"))
    return jax.shard_map(body, mesh=mesh, in_specs=in_specs, out_specs=out_specs, check_vma=False)
```
